512 devices in a mesh: node: 32 (over z, core), local: 16 (over x, y).
Axes of the slice: x: 4, y: 4, z: 16, core: 2. Of those that a mesh axis runs over, the one named last changes fastest.
Arguments:
- populations: float32 [512, 19, 4096], P(('node', 'local')), may hold values from 0.25 to 2.5, as said below
- fluid: int32 [512, 4096], P(('node', 'local')), may hold values 0 or 1
- neighbours: int32 [512, 6], P(('node', 'local')), may hold values from -1 to 511, as said below
Outputs:
- populations_out: float32 [512, 19, 4096], P(('node', 'local'))
- flow: float32 [3], replicated
The draws below stay inside these ranges and needn't reach their ends.
Inputs may be any that keep to these rules, and one draw needn't show every extreme that they name: `populations`: every entry is positive. neighbours[b, k] is -1 or a block n other than b with neighbours[n, k ^ 1] = b; the owners b // 1 and n // 1 differ by at most 2, and by exactly 2 for some pairs.
All inputs are finite; a program needn't handle non-finite values. No bound on the sum of `fluid` on one device may be relied on, other than what follows from the above.
Results may differ from the reference program's by a relative error of at most 0.0003.
Values sent between devices are 32-bit elements; how exact they have to be, the bound alone decides.
No kernel may reach another device: no remote copies, remote signals or barrier semaphores. Data moves between devices by JAX's collectives and lax.ppermute only.
A program may use at most 64 MiB of HBM per device.

```python
import jax
import jax.numpy as jnp
import numpy as np
from jax import lax

BLK = 16
B_DEV = 1
R = 2
SUBSTEPS = 2
NB = 512
CELLS = 4096


VELOCITIES = ((0, 0, 0), (1, 0, 0), (-1, 0, 0), (0, 1, 0), (0, -1, 0), (0, 0, 1), (0, 0, -1), (1, 1, 0), (-1, -1, 0), (1, -1, 0), (-1, 1, 0), (1, 0, 1), (-1, 0, -1), (1, 0, -1), (-1, 0, 1), (0, 1, 1), (0, -1, -1), (0, 1, -1), (0, -1, 1))


def draw_populations(key, part):
    key = jax.random.fold_in(key, 11)
    key_one, key_two, key_three = jax.random.split(key, 3)
    position = jnp.arange(NB, dtype=jnp.float32) / max(NB - 1, 1)
    rising = 1.0 + 2.0 * position
    amplitude = 0.02
    rough = jnp.clip(jax.random.normal(key_one, (NB, 19, CELLS), jnp.float32), -2.0, 2.0) * 0.5
    jitter = jnp.clip(jax.random.normal(key_two, (NB, 3, CELLS), jnp.float32), -2.0, 2.0) * 0.01
    density = jnp.clip(jax.random.normal(key_three, (NB, CELLS), jnp.float32), -2.0, 2.0) * 0.04
    heading = jnp.array([1.0, 0.6, -0.4], dtype=jnp.float32)
    velocity = amplitude * rising[:, None, None] * heading[None, :, None] + jitter
    lattice = jnp.array(VELOCITIES, dtype=jnp.float32)
    project = lattice[:, 0][None, :, None] * velocity[:, 0][:, None, :] + lattice[:, 1][None, :, None] * velocity[:, 1][:, None, :] + lattice[:, 2][None, :, None] * velocity[:, 2][:, None, :]
    speed_sq = velocity[:, 0] * velocity[:, 0] + velocity[:, 1] * velocity[:, 1] + velocity[:, 2] * velocity[:, 2]
    shape_eq = 1.0 + 3.0 * project + 4.5 * project * project - 1.5 * speed_sq[:, None, :]
    return ((1.0 + density)[:, None, :] * shape_eq * (1.0 + 0.25 * rough)).astype(jnp.float32)


def window_order(key, window_id):
    blocks = jnp.arange(NB, dtype=jnp.int32)
    scores = jax.random.randint(key, (NB,), 0, max((1 << 30) // NB, 2)) * NB + blocks
    first = jnp.argsort(scores, stable=True)
    second = jnp.argsort(window_id[first], stable=True)
    return first[second].astype(jnp.int32)


def force_pair(order, source, target):
    where_target = jnp.argmax(order == target).astype(jnp.int32)
    held = order[source]
    order = order.at[where_target].set(held)
    return order.at[source].set(target)


def draw_neighbours(key, part):
    key = jax.random.fold_in(key, 23)
    key_link, key_shift, key_zero, key_one, key_two = jax.random.split(key, 5)
    blocks = jnp.arange(NB, dtype=jnp.int32)
    owners = blocks // B_DEV
    devices = NB // B_DEV
    span = R + 1
    offset = jax.random.randint(key_shift, (), 0, span)
    last_start = (devices - 1 - R) * B_DEV
    linked = jax.random.randint(key_link, (NB, 3), 0, 4) < 3
    linked = linked.at[0, 0].set(True).at[last_start, 1].set(True).at[0, 2].set(False)
    order_zero = force_pair(window_order(key_zero, owners // span), 0, R * B_DEV)
    order_one = force_pair(window_order(key_one, (devices - 1) // span - (devices - 1 - owners) // span), last_start, NB - 1)
    order_two = window_order(key_two, (owners + offset) // span)
    columns = []
    for dim_num, order in enumerate((order_zero, order_one, order_two)):
        valid = linked[:, dim_num] & (order != blocks)
        high_side = jnp.where(valid, order, -1)
        low_side = jnp.full((NB,), -1, jnp.int32).at[order].set(jnp.where(valid, blocks, -1))
        columns.append(low_side)
        columns.append(high_side)
    return jnp.stack(columns, axis=1).astype(jnp.int32)


def plant(drawn, rng, smallest, high):
    longest = drawn.shape.index(max(drawn.shape))
    spots = []
    for shift in (0, 1):
        where = [jax.random.randint(jax.random.fold_in(rng, axis), (), 0, length) for axis, length in enumerate(drawn.shape)]
        where[longest] = (where[longest] + shift) % drawn.shape[longest]
        spots.append(tuple(where))
    return drawn.at[spots[0]].set(smallest).at[spots[1]].set(high)


def setup_inputs(seed: int = 0) -> dict:
    key_list = jax.random.split(jax.random.key(seed), 4)
    populations = draw_populations(jax.random.fold_in(key_list[3], 71), 0)
    fluid = plant((jax.random.randint(key_list[1], (NB, CELLS), 0, 4) < 3).astype(jnp.int32), jax.random.fold_in(key_list[1], 1), 0, 1)
    neighbours = draw_neighbours(jax.random.fold_in(key_list[3], 71), 0)
    return dict(populations=populations, fluid=fluid, neighbours=neighbours)


VELOCITIES = ((0, 0, 0), (1, 0, 0), (-1, 0, 0), (0, 1, 0), (0, -1, 0), (0, 0, 1), (0, 0, -1),
              (1, 1, 0), (-1, -1, 0), (1, -1, 0), (-1, 1, 0), (1, 0, 1), (-1, 0, -1), (1, 0, -1),
              (-1, 0, 1), (0, 1, 1), (0, -1, -1), (0, 1, -1), (0, -1, 1))
WEIGHTS = (1.0 / 3.0,) + (1.0 / 18.0,) * 6 + (1.0 / 36.0,) * 12
OPPOSITE = (0, 2, 1, 4, 3, 6, 5, 8, 7, 10, 9, 12, 11, 14, 13, 16, 15, 18, 17)
OMEGA_PLUS = 1.6
MAGIC_PARAM = 0.1875


def outgoing(which_face):
    dim_num = which_face // 2
    sign_val = 1 if which_face % 2 else -1
    return [direction for direction in range(19) if VELOCITIES[direction][dim_num] == sign_val]


def collide(current, fluid):
    weights = jnp.array(WEIGHTS, dtype=jnp.float32)[:, None]
    lattice = jnp.array(VELOCITIES, dtype=jnp.float32)
    distribution = current * weights
    density = jnp.sum(distribution, axis=1)
    momentum = jnp.einsum("bic,id->bdc", distribution, lattice, precision=lax.Precision.HIGHEST)
    density_safe = jnp.where(fluid > 0, density, 1.0)
    velocity = momentum / density_safe[:, None, :]
    project = jnp.einsum("id,bdc->bic", lattice, velocity, precision=lax.Precision.HIGHEST)
    speed_sq = jnp.sum(velocity * velocity, axis=1)
    equilib = weights * density[:, None, :] * (1.0 + 3.0 * project + 4.5 * project * project - 1.5 * speed_sq[:, None, :])
    reverse = np.array(OPPOSITE)
    dist_rev = distribution[:, reverse]
    equil_rev = equilib[:, reverse]
    omega_minus = 1.0 / (MAGIC_PARAM / (1.0 / OMEGA_PLUS - 0.5) + 0.5)
    collided = (distribution - 0.5 * OMEGA_PLUS * ((distribution + dist_rev) - (equilib + equil_rev))
                - 0.5 * omega_minus * ((distribution - dist_rev) - (equilib - equil_rev)))
    return collided / weights


def face_tiles(collided, fluid, edge_len):
    blocks_here = collided.shape[0]
    cube = collided.reshape(blocks_here, 19, edge_len, edge_len, edge_len)
    wet_cube = fluid.reshape(blocks_here, edge_len, edge_len, edge_len).astype(jnp.float32)
    face_vals = []
    face_wet = []
    for face_num in range(6):
        dim_num = face_num // 2
        layer_at = edge_len - 1 if face_num % 2 else 0
        face_sheet = lax.index_in_dim(cube, layer_at, axis=2 + dim_num, keepdims=False)
        face_vals.append(face_sheet[:, np.array(outgoing(face_num))].reshape(blocks_here, 5, edge_len * edge_len))
        wet_sheet = lax.index_in_dim(wet_cube, layer_at, axis=1 + dim_num, keepdims=False)
        face_wet.append(wet_sheet.reshape(blocks_here, edge_len * edge_len))
    return jnp.stack(face_vals, axis=1), jnp.stack(face_wet, axis=1)


def place_sheet(sheet_vals, dim_num, at_low, edge_len):
    blocks_here = sheet_vals.shape[0]
    sheet_grid = jnp.expand_dims(sheet_vals.reshape(blocks_here, edge_len, edge_len), 1 + dim_num)
    widths = [(0, 0)] * 4
    widths[1 + dim_num] = (0, edge_len - 1) if at_low else (edge_len - 1, 0)
    return jnp.pad(sheet_grid, widths).reshape(blocks_here, edge_len ** 3)


def stream_cells(collided, fluid, tiles_in, wet_in, edge_len):
    cell_count = edge_len ** 3
    positions = np.arange(cell_count)
    coords = (positions // (edge_len * edge_len), (positions // edge_len) % edge_len, positions % edge_len)
    strides = (edge_len * edge_len, edge_len, 1)
    wet_cell = fluid > 0
    outputs = []
    for direction in range(19):
        lattice_vec = VELOCITIES[direction]
        if direction == 0:
            pulled = collided[:, 0]
        else:
            shift_cells = sum(lattice_vec[dim_num] * strides[dim_num] for dim_num in range(3))
            outside = [(coords[dim_num] - lattice_vec[dim_num] < 0) | (coords[dim_num] - lattice_vec[dim_num] >= edge_len) for dim_num in range(3)]
            out_count = outside[0].astype(np.int32) + outside[1].astype(np.int32) + outside[2].astype(np.int32)
            inside = jnp.asarray(out_count == 0)
            source_wet = jnp.roll(wet_cell, shift_cells, axis=1)
            pulled = jnp.where(inside[None, :] & source_wet, jnp.roll(collided[:, direction], shift_cells, axis=1), collided[:, OPPOSITE[direction]])
            for dim_num in range(3):
                if lattice_vec[dim_num] != 0:
                    at_low = lattice_vec[dim_num] > 0
                    face_num = 2 * dim_num + (0 if at_low else 1)
                    slot_index = outgoing(face_num ^ 1).index(direction)
                    crossing = jnp.asarray((out_count == 1) & outside[dim_num])
                    plane_shift = shift_cells - lattice_vec[dim_num] * strides[dim_num]
                    ghost_vals = jnp.roll(place_sheet(tiles_in[:, face_num, slot_index], dim_num, at_low, edge_len), plane_shift, axis=1)
                    ghost_wet = jnp.roll(place_sheet(wet_in[:, face_num], dim_num, at_low, edge_len), plane_shift, axis=1)
                    pulled = jnp.where(crossing[None, :] & (ghost_wet > 0.5), ghost_vals, pulled)
        outputs.append(jnp.where(wet_cell, pulled, 0.0))
    return jnp.stack(outputs, axis=1)


def collide_faces(pair):
    return face_tiles(collide(pair[0], pair[1]), pair[1], BLK)


def collide_stream(group):
    return stream_cells(collide(group[0], group[1]), group[1], group[2], group[3], BLK)


def reference(populations, fluid, neighbours):
    plane = BLK * BLK
    face_from = jnp.array([1, 0, 3, 2, 5, 4], dtype=jnp.int32)
    present = neighbours >= 0
    source_block = jnp.where(present, neighbours, 0).astype(jnp.int32)
    fluid_batches = fluid.reshape(-1, B_DEV, CELLS)
    current = populations
    for substep in range(SUBSTEPS):
        batches = current.reshape(-1, B_DEV, 19, CELLS)
        face_vals, face_wet = lax.map(collide_faces, (batches, fluid_batches))
        face_vals = face_vals.reshape(NB, 6, 5, plane)
        face_wet = face_wet.reshape(NB, 6, plane)
        tiles_in = face_vals[source_block, face_from[None, :]]
        wet_in = face_wet[source_block, face_from[None, :]] * present[:, :, None].astype(jnp.float32)
        current = lax.map(collide_stream,
                          (batches, fluid_batches,
                           tiles_in.reshape(-1, B_DEV, 6, 5, plane),
                           wet_in.reshape(-1, B_DEV, 6, plane))).reshape(NB, 19, CELLS)
    weights = jnp.array(WEIGHTS, dtype=jnp.float32)
    lattice = jnp.array(VELOCITIES, dtype=jnp.float32)
    direction_sums = jnp.sum(current, axis=(0, 2)) * weights
    flow = jnp.dot(lattice.T, direction_sums, precision=lax.Precision.HIGHEST) / (NB * BLK * BLK)
    return current, flow
```

```python
import functools

import jax
import jax.numpy as jnp
from jax import lax
from jax.experimental import pallas as pl
from jax.experimental.pallas import tpu as pltpu
from jax.sharding import PartitionSpec as P

BLK = 16
R = 2

VELOCITIES = (
    (0, 0, 0),
    (1, 0, 0),
    (-1, 0, 0),
    (0, 1, 0),
    (0, -1, 0),
    (0, 0, 1),
    (0, 0, -1),
    (1, 1, 0),
    (-1, -1, 0),
    (1, -1, 0),
    (-1, 1, 0),
    (1, 0, 1),
    (-1, 0, -1),
    (1, 0, -1),
    (-1, 0, 1),
    (0, 1, 1),
    (0, -1, -1),
    (0, 1, -1),
    (0, -1, 1),
)
WEIGHTS = (1.0 / 3.0,) + (1.0 / 18.0,) * 6 + (1.0 / 36.0,) * 12
OPPOSITE = (0, 2, 1, 4, 3, 6, 5, 8, 7, 10, 9, 12, 11, 14, 13, 16, 15, 18, 17)
OMEGA_PLUS = 1.6
MAGIC_PARAM = 0.1875
OMEGA_MINUS = 1.0 / (MAGIC_PARAM / (1.0 / OMEGA_PLUS - 0.5) + 0.5)
STRIDES = (256, 16, 1)

ROWS, LANES = 32, 128
PACK_ROWS = 88
Y_AT, Z_AT, X_LOW_AT, X_HIGH_AT = 0, 32, 64, 76
WET_SLOT = 5
BIG = 3.0e38
LIMIT = 1.0e38


def outgoing(face):
    sign = 1 if face % 2 else -1
    return [i for i in range(19) if VELOCITIES[i][face // 2] == sign]


class Grid:
    def __init__(self):
        self.row = lax.broadcasted_iota(jnp.int32, (ROWS, LANES), 0)
        self.lane = lax.broadcasted_iota(jnp.int32, (ROWS, LANES), 1)
        self.flat = self.row * LANES + self.lane
        self.odd = (self.row & 1) == 1
        self.z = self.lane & 15
        self.slot = self.lane >> 4

    def plane(self, dim, sign):
        if dim == 1:
            return self.odd & (self.slot == 7) if sign > 0 else (~self.odd) & (self.slot == 0)
        return self.z == (15 if sign > 0 else 0)

    def beyond(self, dim, sign, other, other_sign):
        source = (self.flat + sign * STRIDES[dim]) & 4095
        coord = source >> 8 if other == 0 else (source >> 4) & 15
        return coord != (15 if other_sign > 0 else 0)


def lane_roll(a, t):
    t %= LANES
    return a if t == 0 else pltpu.roll(a, t, 1)


def row_roll(a, q):
    q %= ROWS
    return a if q == 0 else pltpu.roll(a, q, 0)


def flat_roll(grid, a, shift):
    q, t = divmod(shift % 4096, LANES)
    if t == 0:
        return row_roll(a, q)
    rolled = lane_roll(a, t)
    return jnp.where(grid.lane >= t, row_roll(rolled, q), row_roll(rolled, q + 1))


def collide(g, wet):
    rho = g[0] * WEIGHTS[0]
    rho = rho + (g[1] + g[2] + g[3] + g[4] + g[5] + g[6]) * WEIGHTS[1]
    diagonal = g[7]
    for i in range(8, 19):
        diagonal = diagonal + g[i]
    rho = rho + diagonal * WEIGHTS[7]
    inverse = 1.0 / jnp.where(wet, rho, 1.0)
    u = []
    for dim in range(3):
        axis_part = diag_part = None
        for i in range(1, 19, 2):
            c = VELOCITIES[i][dim]
            if c == 0:
                continue
            diff = g[i] - g[i + 1] if c > 0 else g[i + 1] - g[i]
            if i < 7:
                axis_part = diff
            else:
                diag_part = diff if diag_part is None else diag_part + diff
        u.append((axis_part * WEIGHTS[1] + diag_part * WEIGHTS[7]) * inverse)
    speed_sq = u[0] * u[0] + u[1] * u[1] + u[2] * u[2]
    base = 1.0 - 1.5 * speed_sq
    out = [None] * 19
    out[0] = g[0] - (0.5 * OMEGA_PLUS) * (2.0 * g[0] - 2.0 * rho * base)
    for i in range(1, 19, 2):
        project = None
        for dim in range(3):
            c = VELOCITIES[i][dim]
            if c > 0:
                project = u[dim] if project is None else project + u[dim]
            elif c < 0:
                project = project - u[dim]
        even = (0.5 * OMEGA_PLUS) * ((g[i] + g[i + 1]) - 2.0 * rho * (base + 4.5 * project * project))
        odd = (0.5 * OMEGA_MINUS) * ((g[i] - g[i + 1]) - 6.0 * rho * project)
        out[i] = g[i] - even - odd
        out[i + 1] = g[i + 1] - even + odd
    return out


def write_pack(grid, g, wet, pack_ref):
    wet_value = jnp.where(wet, 1.0, 0.0)

    def of(face):
        return [g[i] for i in outgoing(face)] + [wet_value]

    low, high = of(2), of(3)
    pack = jnp.zeros((ROWS, LANES), jnp.float32)
    for j in range(6):
        both = jnp.where(grid.odd, lane_roll(high[j], 16 * (j + 1)), lane_roll(low[j], 16 * j))
        pack = jnp.where(grid.slot == j, both, pack)
    pack_ref[Y_AT : Y_AT + ROWS, :] = jnp.where(grid.odd, row_roll(pack, -2), row_roll(pack, 2))
    low, high = of(4), of(5)
    pack = jnp.zeros((ROWS, LANES), jnp.float32)
    for j in range(6):
        pack = jnp.where(grid.z == j, lane_roll(low[j], j), pack)
        pack = jnp.where(grid.z == 8 + j, lane_roll(high[j], j - 7), pack)
    pack_ref[Z_AT : Z_AT + ROWS, :] = jnp.where(
        grid.z >= 8, flat_roll(grid, pack, -16), flat_roll(grid, pack, 16)
    )
    low, high = of(0), of(1)
    for j in range(6):
        pack_ref[X_LOW_AT + 2 * j : X_LOW_AT + 2 * j + 2, :] = low[j][0:2, :]
        pack_ref[X_HIGH_AT + 2 * j : X_HIGH_AT + 2 * j + 2, :] = high[j][30:32, :]


def pair_mate(me):
    return me ^ 1


def other_side(me):
    return ((me + 1) ^ 1) - 1


def pull(grid, wet, own_ref, nb_ref, pack_refs, work_ref, put):
    me = lax.axis_index("node") * lax.axis_size("local") + lax.axis_index("local")
    sources = [other_side(me), pair_mate(me), other_side(pair_mate(me)), pair_mate(other_side(me))]

    def select(face, start, rows):
        block = nb_ref[0, face]
        value = jnp.zeros((rows, LANES), jnp.float32)
        for source, ref in zip(sources, pack_refs):
            value = jnp.where((block >= 0) & (block == source), ref[start : start + rows, :], value)
        return value

    ghost_y = jnp.where(grid.odd, select(2, Y_AT, ROWS), select(3, Y_AT, ROWS))
    ghost_z = jnp.where(grid.z >= 8, select(4, Z_AT, ROWS), select(5, Z_AT, ROWS))
    ghost_x = {1: select(0, X_HIGH_AT, 12), -1: select(1, X_LOW_AT, 12)}
    wet_y = {
        1: lane_roll(ghost_y, 112 - 16 * WET_SLOT) > 0.5,
        -1: lane_roll(ghost_y, -16 * WET_SLOT) > 0.5,
    }
    wet_z = {
        1: lane_roll(ghost_z, 7 - WET_SLOT) > 0.5,
        -1: lane_roll(ghost_z, -WET_SLOT) > 0.5,
    }
    wet_x = {s: ghost_x[s][2 * WET_SLOT : 2 * WET_SLOT + 2, :] > 0.5 for s in (1, -1)}
    put(0, jnp.where(wet, own_ref[0], 0.0), None)
    for i in range(1, 19):
        c = VELOCITIES[i]
        a = own_ref[i]
        if c[0] != 0:
            j = outgoing(1 if c[0] > 0 else 0).index(i)
            at = 30 if c[0] > 0 else 0
            work_ref[i] = a
            work_ref[i, at : at + 2, :] = jnp.where(
                wet_x[c[0]], ghost_x[c[0]][2 * j : 2 * j + 2, :], BIG
            )
            a = work_ref[i]
        if c[1] != 0:
            j = outgoing(3 if c[1] > 0 else 2).index(i)
            ghost = lane_roll(ghost_y, 112 - 16 * j if c[1] > 0 else -16 * j)
            fine = wet_y[c[1]]
            if c[0] != 0:
                fine = fine & grid.beyond(1, c[1], 0, c[0])
            a = jnp.where(grid.plane(1, c[1]), jnp.where(fine, ghost, BIG), a)
        if c[2] != 0:
            j = outgoing(5 if c[2] > 0 else 4).index(i)
            ghost = lane_roll(ghost_z, 7 - j if c[2] > 0 else -j)
            fine = wet_z[c[2]]
            for other in (0, 1):
                if c[other] != 0:
                    fine = fine & grid.beyond(2, c[2], other, c[other])
            a = jnp.where(grid.plane(2, c[2]), jnp.where(fine, ghost, BIG), a)
        moved = flat_roll(grid, a, sum(c[d] * STRIDES[d] for d in range(3)))
        open_link = moved < LIMIT
        value = jnp.where(open_link, moved, own_ref[OPPOSITE[i]])
        put(i, jnp.where(wet, value, 0.0), open_link)


def first_kernel(pop_hbm, fluid_hbm, post_ref, pack_ref, pop_ref, fluid_ref, sems):
    pop_copy = pltpu.make_async_copy(pop_hbm, pop_ref, sems.at[0])
    fluid_copy = pltpu.make_async_copy(fluid_hbm, fluid_ref, sems.at[1])
    pop_copy.start()
    fluid_copy.start()
    fluid_copy.wait()
    pop_copy.wait()
    grid = Grid()
    wet = fluid_ref[...] > 0
    g = collide([pop_ref[i] for i in range(19)], wet)
    for i in range(19):
        post_ref[i] = jnp.where(wet, g[i], BIG)
    write_pack(grid, g, wet, pack_ref)


def pack_kernel(post_ref, fluid_ref, pack_ref):
    wet = fluid_ref[...] > 0
    write_pack(Grid(), [jnp.where(wet, post_ref[i], 0.0) for i in range(19)], wet, pack_ref)


def middle_kernel(own_ref, fluid_ref, nb_ref, p0, p1, p2, p3, post_ref, sum_ref, work_ref, now_ref, sign_ref):
    grid = Grid()
    wet = fluid_ref[...] > 0

    def put(i, value, open_link):
        now_ref[i] = value
        if i:
            sign_ref[i] = jnp.where(wet, jnp.where(open_link, 1.0, -1.0), 0.0)

    pull(grid, wet, own_ref, nb_ref, (p0, p1, p2, p3), work_ref, put)
    g = collide([now_ref[i] for i in range(19)], wet)
    for i in range(19):
        post_ref[i] = jnp.where(wet, g[i], BIG)
    totals = [None] * 3
    for i in range(1, 19, 2):
        signed = (g[i] * sign_ref[i + 1] - g[i + 1] * sign_ref[i]) * WEIGHTS[i]
        for dim in range(3):
            c = VELOCITIES[i][dim]
            if c > 0:
                totals[dim] = signed if totals[dim] is None else totals[dim] + signed
            elif c < 0:
                totals[dim] = -signed if totals[dim] is None else totals[dim] - signed
    lane = lax.broadcasted_iota(jnp.int32, sum_ref.shape, 2)
    line = jnp.zeros(sum_ref.shape, jnp.float32)
    for dim in range(3):
        total = jnp.sum(jnp.sum(totals[dim], axis=0, keepdims=True), axis=1, keepdims=True)[None]
        line = jnp.where(lane == dim, total, line)
    sum_ref[...] = line


def last_kernel(own_ref, fluid_ref, nb_ref, p0, p1, p2, p3, out_ref, work_ref):
    grid = Grid()
    wet = fluid_ref[...] > 0

    def put(i, value, open_link):
        out_ref[i] = value

    pull(grid, wet, own_ref, nb_ref, (p0, p1, p2, p3), work_ref, put)


def vmem(count):
    return [pl.BlockSpec(memory_space=pltpu.VMEM)] * count


def swap(pack, partner):
    length = lax.axis_size("node") * lax.axis_size("local")
    pairs = [(i, partner(i)) for i in range(length) if 0 <= partner(i) < length]
    return lax.ppermute(pack, ("node", "local"), pairs)


def exchange(pack):
    other = swap(pack, other_side)
    mate = swap(pack, pair_mate)
    return [other, mate]


def pass_on(other, mate):
    past_mate = swap(other, pair_mate)
    past_other = swap(mate, other_side)
    return [other, mate, past_mate, past_other]


def spread_out(lines, axis):
    return lax.all_to_all(lines, axis, 0, 0, tiled=True)


def shards(populations, fluid, neighbours):
    f32 = jnp.float32
    cube = jax.ShapeDtypeStruct((19, ROWS, LANES), f32)
    packed = jax.ShapeDtypeStruct((PACK_ROWS, LANES), f32)
    lines = jax.ShapeDtypeStruct((lax.axis_size("local"), 8, LANES), f32)
    scratch = pltpu.VMEM((19, ROWS, LANES), f32)
    smem = [pl.BlockSpec(memory_space=pltpu.SMEM)]
    devices = lax.axis_size("node") * lax.axis_size("local")
    params = pltpu.CompilerParams(vmem_limit_bytes=16 * 2**20)
    pop = populations.reshape(19, ROWS, LANES)
    wall = fluid.reshape(ROWS, LANES)

    post, pack = pl.pallas_call(
        first_kernel,
        out_shape=(cube, packed),
        in_specs=[pl.BlockSpec(memory_space=pltpu.HBM)] * 2,
        out_specs=tuple(vmem(2)),
        scratch_shapes=[scratch, pltpu.VMEM((ROWS, LANES), jnp.int32), pltpu.SemaphoreType.DMA((2,))],
        compiler_params=params,
        name="collide_first",
    )(pop, wall)
    ghosts = pass_on(*exchange(pack))
    post, sums = pl.pallas_call(
        middle_kernel,
        out_shape=(cube, lines),
        in_specs=vmem(2) + smem + vmem(4),
        out_specs=tuple(vmem(2)),
        scratch_shapes=[scratch] * 3,
        compiler_params=params,
        name="stream_collide",
    )(post, wall, neighbours, *ghosts)
    sums = spread_out(sums, "local")
    pack = pl.pallas_call(
        pack_kernel,
        out_shape=packed,
        in_specs=vmem(2),
        out_specs=vmem(1)[0],
        compiler_params=params,
        name="pack_faces",
        cost_estimate=pl.CostEstimate(flops=2000000, bytes_accessed=400000, transcendentals=0),
    )(post, wall)
    other, mate = exchange(pack)
    sums, mate = lax.optimization_barrier((sums, mate))
    plane = jnp.sum(sums[:, 0, :], axis=0, keepdims=True)
    sums = spread_out(jnp.broadcast_to(plane, (lax.axis_size("node"), LANES)), "node")
    ghosts = pass_on(other, mate)
    out = pl.pallas_call(
        last_kernel,
        out_shape=cube,
        in_specs=vmem(2) + smem + vmem(4),
        out_specs=vmem(1)[0],
        scratch_shapes=[scratch],
        compiler_params=params,
        name="stream_last",
        cost_estimate=pl.CostEstimate(flops=4000000, bytes_accessed=1000000, transcendentals=0),
    )(post, wall, neighbours, *ghosts)
    flow = jnp.sum(sums, axis=0)[:3] / (devices * BLK * BLK)
    return out.reshape(populations.shape), flow


def solution(mesh):
    in_specs = (
        P(("node", "local"), None, None),
        P(("node", "local"), None),
        P(("node", "local"), None),
    )
    out_specs = (P(("node", "local"), None, None), P())
    return jax.shard_map(shards, mesh=mesh, in_specs=in_specs, out_specs=out_specs, check_vma=False)
```

```python
import functools

import jax
import jax.numpy as jnp
from jax import lax
from jax.experimental import pallas as pl
from jax.experimental.pallas import tpu as pltpu
from jax.sharding import PartitionSpec as P

BLK = 16
R = 2

VELOCITIES = (
    (0, 0, 0),
    (1, 0, 0),
    (-1, 0, 0),
    (0, 1, 0),
    (0, -1, 0),
    (0, 0, 1),
    (0, 0, -1),
    (1, 1, 0),
    (-1, -1, 0),
    (1, -1, 0),
    (-1, 1, 0),
    (1, 0, 1),
    (-1, 0, -1),
    (1, 0, -1),
    (-1, 0, 1),
    (0, 1, 1),
    (0, -1, -1),
    (0, 1, -1),
    (0, -1, 1),
)
WEIGHTS = (1.0 / 3.0,) + (1.0 / 18.0,) * 6 + (1.0 / 36.0,) * 12
OPPOSITE = (0, 2, 1, 4, 3, 6, 5, 8, 7, 10, 9, 12, 11, 14, 13, 16, 15, 18, 17)
OMEGA_PLUS = 1.6
MAGIC_PARAM = 0.1875
OMEGA_MINUS = 1.0 / (MAGIC_PARAM / (1.0 / OMEGA_PLUS - 0.5) + 0.5)
STRIDES = (256, 16, 1)

ROWS, LANES = 32, 128
PACK_ROWS = 88
Y_AT, Z_AT, X_LOW_AT, X_HIGH_AT = 0, 32, 64, 76
WET_SLOT = 5
BIG = 3.0e38
LIMIT = 1.0e38


def outgoing(face):
    sign = 1 if face % 2 else -1
    return [i for i in range(19) if VELOCITIES[i][face // 2] == sign]


class Grid:
    def __init__(self):
        self.row = lax.broadcasted_iota(jnp.int32, (ROWS, LANES), 0)
        self.lane = lax.broadcasted_iota(jnp.int32, (ROWS, LANES), 1)
        self.flat = self.row * LANES + self.lane
        self.odd = (self.row & 1) == 1
        self.z = self.lane & 15
        self.slot = self.lane >> 4

    def plane(self, dim, sign):
        if dim == 1:
            return self.odd & (self.slot == 7) if sign > 0 else (~self.odd) & (self.slot == 0)
        return self.z == (15 if sign > 0 else 0)

    def beyond(self, dim, sign, other, other_sign):
        source = (self.flat + sign * STRIDES[dim]) & 4095
        coord = source >> 8 if other == 0 else (source >> 4) & 15
        return coord != (15 if other_sign > 0 else 0)


def lane_roll(a, t):
    t %= LANES
    return a if t == 0 else pltpu.roll(a, t, 1)


def row_roll(a, q):
    q %= ROWS
    return a if q == 0 else pltpu.roll(a, q, 0)


def flat_roll(grid, a, shift):
    q, t = divmod(shift % 4096, LANES)
    if t == 0:
        return row_roll(a, q)
    rolled = lane_roll(a, t)
    return jnp.where(grid.lane >= t, row_roll(rolled, q), row_roll(rolled, q + 1))


def collide(g, wet):
    rho = g[0] * WEIGHTS[0]
    rho = rho + (g[1] + g[2] + g[3] + g[4] + g[5] + g[6]) * WEIGHTS[1]
    diagonal = g[7]
    for i in range(8, 19):
        diagonal = diagonal + g[i]
    rho = rho + diagonal * WEIGHTS[7]
    inverse = 1.0 / jnp.where(wet, rho, 1.0)
    u = []
    for dim in range(3):
        axis_part = diag_part = None
        for i in range(1, 19, 2):
            c = VELOCITIES[i][dim]
            if c == 0:
                continue
            diff = g[i] - g[i + 1] if c > 0 else g[i + 1] - g[i]
            if i < 7:
                axis_part = diff
            else:
                diag_part = diff if diag_part is None else diag_part + diff
        u.append((axis_part * WEIGHTS[1] + diag_part * WEIGHTS[7]) * inverse)
    speed_sq = u[0] * u[0] + u[1] * u[1] + u[2] * u[2]
    base = 1.0 - 1.5 * speed_sq
    out = [None] * 19
    out[0] = g[0] - (0.5 * OMEGA_PLUS) * (2.0 * g[0] - 2.0 * rho * base)
    for i in range(1, 19, 2):
        project = None
        for dim in range(3):
            c = VELOCITIES[i][dim]
            if c > 0:
                project = u[dim] if project is None else project + u[dim]
            elif c < 0:
                project = project - u[dim]
        even = (0.5 * OMEGA_PLUS) * ((g[i] + g[i + 1]) - 2.0 * rho * (base + 4.5 * project * project))
        odd = (0.5 * OMEGA_MINUS) * ((g[i] - g[i + 1]) - 6.0 * rho * project)
        out[i] = g[i] - even - odd
        out[i + 1] = g[i + 1] - even + odd
    return out


def write_pack(grid, g, wet, pack_ref):
    wet_value = jnp.where(wet, 1.0, 0.0)

    def of(face):
        return [g[i] for i in outgoing(face)] + [wet_value]

    low, high = of(2), of(3)
    pack = jnp.zeros((ROWS, LANES), jnp.float32)
    for j in range(6):
        both = jnp.where(grid.odd, lane_roll(high[j], 16 * (j + 1)), lane_roll(low[j], 16 * j))
        pack = jnp.where(grid.slot == j, both, pack)
    pack_ref[Y_AT : Y_AT + ROWS, :] = jnp.where(grid.odd, row_roll(pack, -2), row_roll(pack, 2))
    low, high = of(4), of(5)
    pack = jnp.zeros((ROWS, LANES), jnp.float32)
    for j in range(6):
        pack = jnp.where(grid.z == j, lane_roll(low[j], j), pack)
        pack = jnp.where(grid.z == 8 + j, lane_roll(high[j], j - 7), pack)
    pack_ref[Z_AT : Z_AT + ROWS, :] = jnp.where(
        grid.z >= 8, flat_roll(grid, pack, -16), flat_roll(grid, pack, 16)
    )
    low, high = of(0), of(1)
    for j in range(6):
        pack_ref[X_LOW_AT + 2 * j : X_LOW_AT + 2 * j + 2, :] = low[j][0:2, :]
        pack_ref[X_HIGH_AT + 2 * j : X_HIGH_AT + 2 * j + 2, :] = high[j][30:32, :]


def pair_mate(me):
    return me ^ 1


def other_side(me):
    return ((me + 1) ^ 1) - 1


def pull(grid, wet, own_ref, nb_ref, pack_refs, work_ref, put):
    me = lax.axis_index("node") * lax.axis_size("local") + lax.axis_index("local")
    sources = [other_side(me), pair_mate(me), other_side(pair_mate(me)), pair_mate(other_side(me))]

    def select(face, start, rows):
        block = nb_ref[0, face]
        value = jnp.zeros((rows, LANES), jnp.float32)
        for source, ref in zip(sources, pack_refs):
            value = jnp.where((block >= 0) & (block == source), ref[start : start + rows, :], value)
        return value

    ghost_y = jnp.where(grid.odd, select(2, Y_AT, ROWS), select(3, Y_AT, ROWS))
    ghost_z = jnp.where(grid.z >= 8, select(4, Z_AT, ROWS), select(5, Z_AT, ROWS))
    ghost_x = {1: select(0, X_HIGH_AT, 12), -1: select(1, X_LOW_AT, 12)}
    wet_y = {
        1: lane_roll(ghost_y, 112 - 16 * WET_SLOT) > 0.5,
        -1: lane_roll(ghost_y, -16 * WET_SLOT) > 0.5,
    }
    wet_z = {
        1: lane_roll(ghost_z, 7 - WET_SLOT) > 0.5,
        -1: lane_roll(ghost_z, -WET_SLOT) > 0.5,
    }
    wet_x = {s: ghost_x[s][2 * WET_SLOT : 2 * WET_SLOT + 2, :] > 0.5 for s in (1, -1)}
    put(0, jnp.where(wet, own_ref[0], 0.0), None)
    for i in range(1, 19):
        c = VELOCITIES[i]
        a = own_ref[i]
        if c[0] != 0:
            j = outgoing(1 if c[0] > 0 else 0).index(i)
            at = 30 if c[0] > 0 else 0
            work_ref[i] = a
            work_ref[i, at : at + 2, :] = jnp.where(
                wet_x[c[0]], ghost_x[c[0]][2 * j : 2 * j + 2, :], BIG
            )
            a = work_ref[i]
        if c[1] != 0:
            j = outgoing(3 if c[1] > 0 else 2).index(i)
            ghost = lane_roll(ghost_y, 112 - 16 * j if c[1] > 0 else -16 * j)
            fine = wet_y[c[1]]
            if c[0] != 0:
                fine = fine & grid.beyond(1, c[1], 0, c[0])
            a = jnp.where(grid.plane(1, c[1]), jnp.where(fine, ghost, BIG), a)
        if c[2] != 0:
            j = outgoing(5 if c[2] > 0 else 4).index(i)
            ghost = lane_roll(ghost_z, 7 - j if c[2] > 0 else -j)
            fine = wet_z[c[2]]
            for other in (0, 1):
                if c[other] != 0:
                    fine = fine & grid.beyond(2, c[2], other, c[other])
            a = jnp.where(grid.plane(2, c[2]), jnp.where(fine, ghost, BIG), a)
        moved = flat_roll(grid, a, sum(c[d] * STRIDES[d] for d in range(3)))
        open_link = moved < LIMIT
        value = jnp.where(open_link, moved, own_ref[OPPOSITE[i]])
        put(i, jnp.where(wet, value, 0.0), open_link)


def first_kernel(pop_hbm, fluid_hbm, post_ref, pack_ref, pop_ref, fluid_ref, sems):
    pop_copy = pltpu.make_async_copy(pop_hbm, pop_ref, sems.at[0])
    fluid_copy = pltpu.make_async_copy(fluid_hbm, fluid_ref, sems.at[1])
    pop_copy.start()
    fluid_copy.start()
    fluid_copy.wait()
    pop_copy.wait()
    grid = Grid()
    wet = fluid_ref[...] > 0
    g = collide([pop_ref[i] for i in range(19)], wet)
    for i in range(19):
        post_ref[i] = jnp.where(wet, g[i], BIG)
    write_pack(grid, g, wet, pack_ref)


def pack_kernel(post_ref, fluid_ref, pack_ref):
    wet = fluid_ref[...] > 0
    write_pack(Grid(), [jnp.where(wet, post_ref[i], 0.0) for i in range(19)], wet, pack_ref)


def middle_kernel(own_ref, fluid_ref, nb_ref, p0, p1, p2, p3, post_ref, sum_ref, work_ref, now_ref, sign_ref):
    grid = Grid()
    wet = fluid_ref[...] > 0

    def put(i, value, open_link):
        now_ref[i] = value
        if i:
            sign_ref[i] = jnp.where(wet, jnp.where(open_link, 1.0, -1.0), 0.0)

    pull(grid, wet, own_ref, nb_ref, (p0, p1, p2, p3), work_ref, put)
    g = collide([now_ref[i] for i in range(19)], wet)
    for i in range(19):
        post_ref[i] = jnp.where(wet, g[i], BIG)
    totals = [None] * 3
    for i in range(1, 19, 2):
        signed = (g[i] * sign_ref[i + 1] - g[i + 1] * sign_ref[i]) * WEIGHTS[i]
        for dim in range(3):
            c = VELOCITIES[i][dim]
            if c > 0:
                totals[dim] = signed if totals[dim] is None else totals[dim] + signed
            elif c < 0:
                totals[dim] = -signed if totals[dim] is None else totals[dim] - signed
    lane = lax.broadcasted_iota(jnp.int32, sum_ref.shape, 2)
    line = jnp.zeros(sum_ref.shape, jnp.float32)
    for dim in range(3):
        total = jnp.sum(jnp.sum(totals[dim], axis=0, keepdims=True), axis=1, keepdims=True)[None]
        line = jnp.where(lane == dim, total, line)
    sum_ref[...] = line


def last_kernel(own_ref, fluid_ref, nb_ref, p0, p1, p3, p2, sum_ref, out_ref, flow_ref, work_ref):
    grid = Grid()
    total = jnp.sum(sum_ref[...], axis=0, keepdims=True)
    lane = lax.broadcasted_iota(jnp.int32, (1, LANES), 1)
    cells = lax.axis_size("node") * lax.axis_size("local") * BLK * BLK
    for dim in range(3):
        flow_ref[dim] = jnp.sum(jnp.where(lane == dim, total, 0.0)) / cells
    wet = fluid_ref[...] > 0

    def put(i, value, open_link):
        out_ref[i] = value

    pull(grid, wet, own_ref, nb_ref, (p0, p1, p2, p3), work_ref, put)


def vmem(count):
    return [pl.BlockSpec(memory_space=pltpu.VMEM)] * count


def swap(pack, partner):
    length = lax.axis_size("node") * lax.axis_size("local")
    pairs = [(i, partner(i)) for i in range(length) if 0 <= partner(i) < length]
    return lax.ppermute(pack, ("node", "local"), pairs)


def exchange(pack):
    other = swap(pack, other_side)
    mate = swap(pack, pair_mate)
    return [other, mate]


def pass_on(other, mate):
    past_mate = swap(other, pair_mate)
    past_other = swap(mate, other_side)
    return [other, mate, past_mate, past_other]


def spread_out(lines, axis):
    return lax.all_to_all(lines, axis, 0, 0, tiled=True)


def shards(populations, fluid, neighbours):
    f32 = jnp.float32
    cube = jax.ShapeDtypeStruct((19, ROWS, LANES), f32)
    packed = jax.ShapeDtypeStruct((PACK_ROWS, LANES), f32)
    lines = jax.ShapeDtypeStruct((lax.axis_size("local"), 4, LANES), f32)
    scratch = pltpu.VMEM((19, ROWS, LANES), f32)
    smem = [pl.BlockSpec(memory_space=pltpu.SMEM)]
    params = pltpu.CompilerParams(vmem_limit_bytes=16 * 2**20)
    pop = populations.reshape(19, ROWS, LANES)
    wall = fluid.reshape(ROWS, LANES)

    post, pack = pl.pallas_call(
        first_kernel,
        out_shape=(cube, packed),
        in_specs=[pl.BlockSpec(memory_space=pltpu.HBM)] * 2,
        out_specs=tuple(vmem(2)),
        scratch_shapes=[scratch, pltpu.VMEM((ROWS, LANES), jnp.int32), pltpu.SemaphoreType.DMA((2,))],
        compiler_params=params,
        name="collide_first",
    )(pop, wall)
    ghosts = pass_on(*exchange(pack))
    post, sums = pl.pallas_call(
        middle_kernel,
        out_shape=(cube, lines),
        in_specs=vmem(2) + smem + vmem(4),
        out_specs=tuple(vmem(2)),
        scratch_shapes=[scratch] * 3,
        compiler_params=params,
        name="stream_collide",
    )(post, wall, neighbours, *ghosts)
    sums = spread_out(sums, "local")
    pack = pl.pallas_call(
        pack_kernel,
        out_shape=packed,
        in_specs=vmem(2),
        out_specs=vmem(1)[0],
        compiler_params=params,
        name="pack_faces",
        cost_estimate=pl.CostEstimate(flops=2000000, bytes_accessed=400000, transcendentals=0),
    )(post, wall)
    other, mate = exchange(pack)
    sums, mate = lax.optimization_barrier((sums, mate))
    plane = jnp.sum(sums[:, 0, :], axis=0, keepdims=True)
    sums = spread_out(jnp.broadcast_to(plane, (lax.axis_size("node"), LANES)), "node")
    other, mate, past_mate, past_other = pass_on(other, mate)
    out, flow = pl.pallas_call(
        last_kernel,
        out_shape=(cube, jax.ShapeDtypeStruct((3,), f32)),
        in_specs=vmem(2) + smem + vmem(5),
        out_specs=tuple(vmem(1) + smem),
        scratch_shapes=[scratch],
        compiler_params=params,
        name="stream_last",
        cost_estimate=pl.CostEstimate(flops=4000000, bytes_accessed=1000000, transcendentals=0),
    )(post, wall, neighbours, other, mate, past_other, past_mate, sums)
    return out.reshape(populations.shape), flow


def solution(mesh):
    in_specs = (
        P(("node", "local"), None, None),
        P(("node", "local"), None),
        P(("node", "local"), None),
    )
    out_specs = (P(("node", "local"), None, None), P())
    return jax.shard_map(shards, mesh=mesh, in_specs=in_specs, out_specs=out_specs, check_vma=False)
```

```python
import functools

import jax
import jax.numpy as jnp
from jax import lax
from jax.experimental import pallas as pl
from jax.experimental.pallas import tpu as pltpu
from jax.sharding import PartitionSpec as P

BLK = 16
R = 2

VELOCITIES = (
    (0, 0, 0),
    (1, 0, 0),
    (-1, 0, 0),
    (0, 1, 0),
    (0, -1, 0),
    (0, 0, 1),
    (0, 0, -1),
    (1, 1, 0),
    (-1, -1, 0),
    (1, -1, 0),
    (-1, 1, 0),
    (1, 0, 1),
    (-1, 0, -1),
    (1, 0, -1),
    (-1, 0, 1),
    (0, 1, 1),
    (0, -1, -1),
    (0, 1, -1),
    (0, -1, 1),
)
WEIGHTS = (1.0 / 3.0,) + (1.0 / 18.0,) * 6 + (1.0 / 36.0,) * 12
OPPOSITE = (0, 2, 1, 4, 3, 6, 5, 8, 7, 10, 9, 12, 11, 14, 13, 16, 15, 18, 17)
OMEGA_PLUS = 1.6
MAGIC_PARAM = 0.1875
OMEGA_MINUS = 1.0 / (MAGIC_PARAM / (1.0 / OMEGA_PLUS - 0.5) + 0.5)
STRIDES = (256, 16, 1)

ROWS, LANES = 32, 128
PACK_ROWS = 88
Y_AT, Z_AT, X_LOW_AT, X_HIGH_AT = 0, 32, 64, 76
WET_SLOT = 5
BIG = 3.0e38
LIMIT = 1.0e38


def outgoing(face):
    sign = 1 if face % 2 else -1
    return [i for i in range(19) if VELOCITIES[i][face // 2] == sign]


class Grid:
    def __init__(self):
        self.row = lax.broadcasted_iota(jnp.int32, (ROWS, LANES), 0)
        self.lane = lax.broadcasted_iota(jnp.int32, (ROWS, LANES), 1)
        self.flat = self.row * LANES + self.lane
        self.odd = (self.row & 1) == 1
        self.z = self.lane & 15
        self.slot = self.lane >> 4

    def plane(self, dim, sign):
        if dim == 1:
            return self.odd & (self.slot == 7) if sign > 0 else (~self.odd) & (self.slot == 0)
        return self.z == (15 if sign > 0 else 0)

    def beyond(self, dim, sign, other, other_sign):
        source = (self.flat + sign * STRIDES[dim]) & 4095
        coord = source >> 8 if other == 0 else (source >> 4) & 15
        return coord != (15 if other_sign > 0 else 0)


def lane_roll(a, t):
    t %= LANES
    return a if t == 0 else pltpu.roll(a, t, 1)


def row_roll(a, q):
    q %= ROWS
    return a if q == 0 else pltpu.roll(a, q, 0)


def flat_roll(grid, a, shift):
    q, t = divmod(shift % 4096, LANES)
    if t == 0:
        return row_roll(a, q)
    rolled = lane_roll(a, t)
    return jnp.where(grid.lane >= t, row_roll(rolled, q), row_roll(rolled, q + 1))


def collide(g, wet):
    rho = g[0] * WEIGHTS[0]
    rho = rho + (g[1] + g[2] + g[3] + g[4] + g[5] + g[6]) * WEIGHTS[1]
    diagonal = g[7]
    for i in range(8, 19):
        diagonal = diagonal + g[i]
    rho = rho + diagonal * WEIGHTS[7]
    inverse = 1.0 / jnp.where(wet, rho, 1.0)
    u = []
    for dim in range(3):
        axis_part = diag_part = None
        for i in range(1, 19, 2):
            c = VELOCITIES[i][dim]
            if c == 0:
                continue
            diff = g[i] - g[i + 1] if c > 0 else g[i + 1] - g[i]
            if i < 7:
                axis_part = diff
            else:
                diag_part = diff if diag_part is None else diag_part + diff
        u.append((axis_part * WEIGHTS[1] + diag_part * WEIGHTS[7]) * inverse)
    speed_sq = u[0] * u[0] + u[1] * u[1] + u[2] * u[2]
    base = 1.0 - 1.5 * speed_sq
    out = [None] * 19
    out[0] = g[0] - (0.5 * OMEGA_PLUS) * (2.0 * g[0] - 2.0 * rho * base)
    for i in range(1, 19, 2):
        project = None
        for dim in range(3):
            c = VELOCITIES[i][dim]
            if c > 0:
                project = u[dim] if project is None else project + u[dim]
            elif c < 0:
                project = project - u[dim]
        even = (0.5 * OMEGA_PLUS) * ((g[i] + g[i + 1]) - 2.0 * rho * (base + 4.5 * project * project))
        odd = (0.5 * OMEGA_MINUS) * ((g[i] - g[i + 1]) - 6.0 * rho * project)
        out[i] = g[i] - even - odd
        out[i + 1] = g[i + 1] - even + odd
    return out


def write_pack(grid, g, wet, pack_ref):
    wet_value = jnp.where(wet, 1.0, 0.0)

    def of(face):
        return [g[i] for i in outgoing(face)] + [wet_value]

    low, high = of(2), of(3)
    pack = jnp.zeros((ROWS, LANES), jnp.float32)
    for j in range(6):
        both = jnp.where(grid.odd, lane_roll(high[j], 16 * (j + 1)), lane_roll(low[j], 16 * j))
        pack = jnp.where(grid.slot == j, both, pack)
    pack_ref[Y_AT : Y_AT + ROWS, :] = jnp.where(grid.odd, row_roll(pack, -2), row_roll(pack, 2))
    low, high = of(4), of(5)
    pack = jnp.zeros((ROWS, LANES), jnp.float32)
    for j in range(6):
        pack = jnp.where(grid.z == j, lane_roll(low[j], j), pack)
        pack = jnp.where(grid.z == 8 + j, lane_roll(high[j], j - 7), pack)
    pack_ref[Z_AT : Z_AT + ROWS, :] = jnp.where(
        grid.z >= 8, flat_roll(grid, pack, -16), flat_roll(grid, pack, 16)
    )
    low, high = of(0), of(1)
    for j in range(6):
        pack_ref[X_LOW_AT + 2 * j : X_LOW_AT + 2 * j + 2, :] = low[j][0:2, :]
        pack_ref[X_HIGH_AT + 2 * j : X_HIGH_AT + 2 * j + 2, :] = high[j][30:32, :]


def pair_mate(me):
    return me ^ 1


def other_side(me):
    return ((me + 1) ^ 1) - 1


def place():
    return lax.axis_index("node") * lax.axis_size("local") + lax.axis_index("local")


def pick(grid, nb_ref, tiles, base_ref=None):
    def select(face, start, rows):
        block = nb_ref[0, face]
        if base_ref is None:
            value = jnp.zeros((rows, LANES), jnp.float32)
        else:
            value = base_ref[start : start + rows, :]
        for source, ref in tiles:
            value = jnp.where((block >= 0) & (block == source), ref[start : start + rows, :], value)
        return value

    ghost_y = jnp.where(grid.odd, select(2, Y_AT, ROWS), select(3, Y_AT, ROWS))
    ghost_z = jnp.where(grid.z >= 8, select(4, Z_AT, ROWS), select(5, Z_AT, ROWS))
    return ghost_y, ghost_z, select(0, X_HIGH_AT, 12), select(1, X_LOW_AT, 12)


def pull(grid, wet, own_ref, nb_ref, tiles, base_ref, work_ref, put):
    ghost_y, ghost_z, low_x, high_x = pick(grid, nb_ref, tiles, base_ref)
    ghost_x = {1: low_x, -1: high_x}
    wet_y = {
        1: lane_roll(ghost_y, 112 - 16 * WET_SLOT) > 0.5,
        -1: lane_roll(ghost_y, -16 * WET_SLOT) > 0.5,
    }
    wet_z = {
        1: lane_roll(ghost_z, 7 - WET_SLOT) > 0.5,
        -1: lane_roll(ghost_z, -WET_SLOT) > 0.5,
    }
    wet_x = {s: ghost_x[s][2 * WET_SLOT : 2 * WET_SLOT + 2, :] > 0.5 for s in (1, -1)}
    put(0, jnp.where(wet, own_ref[0], 0.0), None)
    for i in range(1, 19):
        c = VELOCITIES[i]
        a = own_ref[i]
        if c[0] != 0:
            j = outgoing(1 if c[0] > 0 else 0).index(i)
            at = 30 if c[0] > 0 else 0
            work_ref[i] = a
            work_ref[i, at : at + 2, :] = jnp.where(
                wet_x[c[0]], ghost_x[c[0]][2 * j : 2 * j + 2, :], BIG
            )
            a = work_ref[i]
        if c[1] != 0:
            j = outgoing(3 if c[1] > 0 else 2).index(i)
            ghost = lane_roll(ghost_y, 112 - 16 * j if c[1] > 0 else -16 * j)
            fine = wet_y[c[1]]
            if c[0] != 0:
                fine = fine & grid.beyond(1, c[1], 0, c[0])
            a = jnp.where(grid.plane(1, c[1]), jnp.where(fine, ghost, BIG), a)
        if c[2] != 0:
            j = outgoing(5 if c[2] > 0 else 4).index(i)
            ghost = lane_roll(ghost_z, 7 - j if c[2] > 0 else -j)
            fine = wet_z[c[2]]
            for other in (0, 1):
                if c[other] != 0:
                    fine = fine & grid.beyond(2, c[2], other, c[other])
            a = jnp.where(grid.plane(2, c[2]), jnp.where(fine, ghost, BIG), a)
        moved = flat_roll(grid, a, sum(c[d] * STRIDES[d] for d in range(3)))
        open_link = moved < LIMIT
        value = jnp.where(open_link, moved, own_ref[OPPOSITE[i]])
        put(i, jnp.where(wet, value, 0.0), open_link)


def first_kernel(pop_hbm, fluid_hbm, post_ref, pack_ref, pop_ref, fluid_ref, sems):
    pop_copy = pltpu.make_async_copy(pop_hbm, pop_ref, sems.at[0])
    fluid_copy = pltpu.make_async_copy(fluid_hbm, fluid_ref, sems.at[1])
    pop_copy.start()
    fluid_copy.start()
    fluid_copy.wait()
    pop_copy.wait()
    grid = Grid()
    wet = fluid_ref[...] > 0
    g = collide([pop_ref[i] for i in range(19)], wet)
    for i in range(19):
        post_ref[i] = jnp.where(wet, g[i], BIG)
    write_pack(grid, g, wet, pack_ref)


def middle_kernel(own_ref, fluid_ref, nb_ref, p0, p1, p2, p3, post_ref, pack_ref, sum_hbm, work_ref, now_ref, sign_ref, sum_ref, sem):
    grid = Grid()
    wet = fluid_ref[...] > 0

    def put(i, value, open_link):
        now_ref[i] = value
        if i:
            sign_ref[i] = jnp.where(wet, jnp.where(open_link, 1.0, -1.0), 0.0)

    me = place()
    tiles = (
        (other_side(me), p0),
        (pair_mate(me), p1),
        (other_side(pair_mate(me)), p2),
        (pair_mate(other_side(me)), p3),
    )
    pull(grid, wet, own_ref, nb_ref, tiles, None, work_ref, put)
    g = collide([now_ref[i] for i in range(19)], wet)
    totals = [None] * 3
    for i in range(1, 19, 2):
        signed = (g[i] * sign_ref[i + 1] - g[i + 1] * sign_ref[i]) * WEIGHTS[i]
        for dim in range(3):
            c = VELOCITIES[i][dim]
            if c > 0:
                totals[dim] = signed if totals[dim] is None else totals[dim] + signed
            elif c < 0:
                totals[dim] = -signed if totals[dim] is None else totals[dim] - signed
    lane = lax.broadcasted_iota(jnp.int32, sum_ref.shape, 2)
    line = jnp.zeros(sum_ref.shape, jnp.float32)
    for dim in range(3):
        total = jnp.sum(jnp.sum(totals[dim], axis=0, keepdims=True), axis=1, keepdims=True)[None]
        line = jnp.where(lane == dim, total, line)
    sum_ref[...] = line
    sum_copy = pltpu.make_async_copy(sum_ref, sum_hbm, sem)
    sum_copy.start()
    for i in range(19):
        post_ref[i] = jnp.where(wet, g[i], BIG)
    write_pack(grid, g, wet, pack_ref)
    sum_copy.wait()


def pick_kernel(nb_ref, p0, p1, p3, tile_ref):
    me = place()
    tiles = ((other_side(me), p0), (pair_mate(me), p1), (pair_mate(other_side(me)), p3))
    ghost_y, ghost_z, low_x, high_x = pick(Grid(), nb_ref, tiles)
    tile_ref[Y_AT : Y_AT + ROWS, :] = ghost_y
    tile_ref[Z_AT : Z_AT + ROWS, :] = ghost_z
    tile_ref[X_HIGH_AT : X_HIGH_AT + 12, :] = low_x
    tile_ref[X_LOW_AT : X_LOW_AT + 12, :] = high_x


def last_kernel(own_ref, fluid_ref, nb_ref, base_ref, p2, out_ref, work_ref):
    grid = Grid()
    wet = fluid_ref[...] > 0

    def put(i, value, open_link):
        out_ref[i] = value

    pull(grid, wet, own_ref, nb_ref, ((other_side(pair_mate(place())), p2),), base_ref, work_ref, put)


def vmem(count):
    return [pl.BlockSpec(memory_space=pltpu.VMEM)] * count


def swap(pack, partner):
    length = lax.axis_size("node") * lax.axis_size("local")
    pairs = [(i, partner(i)) for i in range(length) if 0 <= partner(i) < length]
    return lax.ppermute(pack, ("node", "local"), pairs)


def exchange(pack):
    other = swap(pack, other_side)
    mate = swap(pack, pair_mate)
    return [other, mate]


def pass_on(other, mate):
    past_mate = swap(other, pair_mate)
    past_other = swap(mate, other_side)
    return [other, mate, past_mate, past_other]


def spread_out(lines, axis):
    return lax.all_to_all(lines, axis, 0, 0, tiled=True)


def shards(populations, fluid, neighbours):
    f32 = jnp.float32
    cube = jax.ShapeDtypeStruct((19, ROWS, LANES), f32)
    packed = jax.ShapeDtypeStruct((PACK_ROWS, LANES), f32)
    lines = jax.ShapeDtypeStruct((lax.axis_size("local"), 8, LANES), f32)
    scratch = pltpu.VMEM((19, ROWS, LANES), f32)
    smem = [pl.BlockSpec(memory_space=pltpu.SMEM)]
    devices = lax.axis_size("node") * lax.axis_size("local")
    params = pltpu.CompilerParams(vmem_limit_bytes=16 * 2**20)
    pop = populations.reshape(19, ROWS, LANES)
    wall = fluid.reshape(ROWS, LANES)

    post, pack = pl.pallas_call(
        first_kernel,
        out_shape=(cube, packed),
        in_specs=[pl.BlockSpec(memory_space=pltpu.HBM)] * 2,
        out_specs=tuple(vmem(2)),
        scratch_shapes=[scratch, pltpu.VMEM((ROWS, LANES), jnp.int32), pltpu.SemaphoreType.DMA((2,))],
        compiler_params=pltpu.CompilerParams(vmem_limit_bytes=60 * 2**20),
        name="collide_first",
    )(pop, wall)
    ghosts = pass_on(*exchange(pack))
    post, pack, sums = pl.pallas_call(
        middle_kernel,
        out_shape=(cube, packed, lines),
        in_specs=vmem(2) + smem + vmem(4),
        out_specs=tuple(vmem(2)) + (pl.BlockSpec(memory_space=pl.ANY),),
        scratch_shapes=[scratch] * 3 + [pltpu.VMEM(lines.shape, f32), pltpu.SemaphoreType.DMA],
        compiler_params=params,
        name="stream_collide",
    )(post, wall, neighbours, *ghosts)
    sums = spread_out(sums, "local")
    other, mate = exchange(pack)
    sums, mate = lax.optimization_barrier((sums, mate))
    plane = jnp.sum(sums[:, 0, :], axis=0, keepdims=True)
    sums = spread_out(jnp.broadcast_to(plane, (lax.axis_size("node"), LANES)), "node")
    other, mate, past_mate, past_other = pass_on(other, mate)
    tile = pl.pallas_call(
        pick_kernel,
        out_shape=packed,
        in_specs=smem + vmem(3),
        out_specs=vmem(1)[0],
        compiler_params=params,
        name="pick_tiles",
        cost_estimate=pl.CostEstimate(flops=1000000, bytes_accessed=400000, transcendentals=0),
    )(neighbours, other, mate, past_other)
    out = pl.pallas_call(
        last_kernel,
        out_shape=cube,
        in_specs=vmem(2) + smem + vmem(2),
        out_specs=vmem(1)[0],
        scratch_shapes=[scratch],
        compiler_params=params,
        name="stream_last",
        cost_estimate=pl.CostEstimate(flops=4000000, bytes_accessed=1000000, transcendentals=0),
    )(post, wall, neighbours, tile, past_mate)
    flow = jnp.sum(sums, axis=0)[:3] / (devices * BLK * BLK)
    return out.reshape(populations.shape), flow


def solution(mesh):
    in_specs = (
        P(("node", "local"), None, None),
        P(("node", "local"), None),
        P(("node", "local"), None),
    )
    out_specs = (P(("node", "local"), None, None), P())
    return jax.shard_map(shards, mesh=mesh, in_specs=in_specs, out_specs=out_specs, check_vma=False)
```

```python
import functools

import jax
import jax.numpy as jnp
from jax import lax
from jax.experimental import pallas as pl
from jax.experimental.pallas import tpu as pltpu
from jax.sharding import PartitionSpec as P

BLK = 16
R = 2

VELOCITIES = (
    (0, 0, 0),
    (1, 0, 0),
    (-1, 0, 0),
    (0, 1, 0),
    (0, -1, 0),
    (0, 0, 1),
    (0, 0, -1),
    (1, 1, 0),
    (-1, -1, 0),
    (1, -1, 0),
    (-1, 1, 0),
    (1, 0, 1),
    (-1, 0, -1),
    (1, 0, -1),
    (-1, 0, 1),
    (0, 1, 1),
    (0, -1, -1),
    (0, 1, -1),
    (0, -1, 1),
)
WEIGHTS = (1.0 / 3.0,) + (1.0 / 18.0,) * 6 + (1.0 / 36.0,) * 12
OPPOSITE = (0, 2, 1, 4, 3, 6, 5, 8, 7, 10, 9, 12, 11, 14, 13, 16, 15, 18, 17)
OMEGA_PLUS = 1.6
MAGIC_PARAM = 0.1875
OMEGA_MINUS = 1.0 / (MAGIC_PARAM / (1.0 / OMEGA_PLUS - 0.5) + 0.5)
STRIDES = (256, 16, 1)

ROWS, LANES = 32, 128
PACK_ROWS = 88
Y_AT, Z_AT, X_LOW_AT, X_HIGH_AT = 0, 32, 64, 76
WET_SLOT = 5
BIG = 3.0e38
LIMIT = 1.0e38


def outgoing(face):
    sign = 1 if face % 2 else -1
    return [i for i in range(19) if VELOCITIES[i][face // 2] == sign]


class Grid:
    def __init__(self):
        self.row = lax.broadcasted_iota(jnp.int32, (ROWS, LANES), 0)
        self.lane = lax.broadcasted_iota(jnp.int32, (ROWS, LANES), 1)
        self.flat = self.row * LANES + self.lane
        self.odd = (self.row & 1) == 1
        self.z = self.lane & 15
        self.slot = self.lane >> 4

    def plane(self, dim, sign):
        if dim == 1:
            return self.odd & (self.slot == 7) if sign > 0 else (~self.odd) & (self.slot == 0)
        return self.z == (15 if sign > 0 else 0)

    def beyond(self, dim, sign, other, other_sign):
        source = (self.flat + sign * STRIDES[dim]) & 4095
        coord = source >> 8 if other == 0 else (source >> 4) & 15
        return coord != (15 if other_sign > 0 else 0)


def lane_roll(a, t):
    t %= LANES
    return a if t == 0 else pltpu.roll(a, t, 1)


def row_roll(a, q):
    q %= ROWS
    return a if q == 0 else pltpu.roll(a, q, 0)


def flat_roll(grid, a, shift):
    q, t = divmod(shift % 4096, LANES)
    if t == 0:
        return row_roll(a, q)
    rolled = lane_roll(a, t)
    return jnp.where(grid.lane >= t, row_roll(rolled, q), row_roll(rolled, q + 1))


def collide(g, wet):
    rho = g[0] * WEIGHTS[0]
    rho = rho + (g[1] + g[2] + g[3] + g[4] + g[5] + g[6]) * WEIGHTS[1]
    diagonal = g[7]
    for i in range(8, 19):
        diagonal = diagonal + g[i]
    rho = rho + diagonal * WEIGHTS[7]
    inverse = 1.0 / jnp.where(wet, rho, 1.0)
    u = []
    for dim in range(3):
        axis_part = diag_part = None
        for i in range(1, 19, 2):
            c = VELOCITIES[i][dim]
            if c == 0:
                continue
            diff = g[i] - g[i + 1] if c > 0 else g[i + 1] - g[i]
            if i < 7:
                axis_part = diff
            else:
                diag_part = diff if diag_part is None else diag_part + diff
        u.append((axis_part * WEIGHTS[1] + diag_part * WEIGHTS[7]) * inverse)
    speed_sq = u[0] * u[0] + u[1] * u[1] + u[2] * u[2]
    base = 1.0 - 1.5 * speed_sq
    out = [None] * 19
    out[0] = g[0] - (0.5 * OMEGA_PLUS) * (2.0 * g[0] - 2.0 * rho * base)
    for i in range(1, 19, 2):
        project = None
        for dim in range(3):
            c = VELOCITIES[i][dim]
            if c > 0:
                project = u[dim] if project is None else project + u[dim]
            elif c < 0:
                project = project - u[dim]
        even = (0.5 * OMEGA_PLUS) * ((g[i] + g[i + 1]) - 2.0 * rho * (base + 4.5 * project * project))
        odd = (0.5 * OMEGA_MINUS) * ((g[i] - g[i + 1]) - 6.0 * rho * project)
        out[i] = g[i] - even - odd
        out[i + 1] = g[i + 1] - even + odd
    return out


def write_pack(grid, g, wet, pack_ref):
    wet_value = jnp.where(wet, 1.0, 0.0)

    def of(face):
        return [g[i] for i in outgoing(face)] + [wet_value]

    low, high = of(2), of(3)
    pack = jnp.zeros((ROWS, LANES), jnp.float32)
    for j in range(6):
        both = jnp.where(grid.odd, lane_roll(high[j], 16 * (j + 1)), lane_roll(low[j], 16 * j))
        pack = jnp.where(grid.slot == j, both, pack)
    pack_ref[Y_AT : Y_AT + ROWS, :] = jnp.where(grid.odd, row_roll(pack, -2), row_roll(pack, 2))
    low, high = of(4), of(5)
    pack = jnp.zeros((ROWS, LANES), jnp.float32)
    for j in range(6):
        pack = jnp.where(grid.z == j, lane_roll(low[j], j), pack)
        pack = jnp.where(grid.z == 8 + j, lane_roll(high[j], j - 7), pack)
    pack_ref[Z_AT : Z_AT + ROWS, :] = jnp.where(
        grid.z >= 8, flat_roll(grid, pack, -16), flat_roll(grid, pack, 16)
    )
    low, high = of(0), of(1)
    for j in range(6):
        pack_ref[X_LOW_AT + 2 * j : X_LOW_AT + 2 * j + 2, :] = low[j][0:2, :]
        pack_ref[X_HIGH_AT + 2 * j : X_HIGH_AT + 2 * j + 2, :] = high[j][30:32, :]


def pair_mate(me):
    return me ^ 1


def other_side(me):
    return ((me + 1) ^ 1) - 1


def place():
    return lax.axis_index("node") * lax.axis_size("local") + lax.axis_index("local")


def pick(grid, nb_ref, tiles, base_ref=None):
    def select(face, start, rows):
        block = nb_ref[0, face]
        if base_ref is None:
            value = jnp.zeros((rows, LANES), jnp.float32)
        else:
            value = base_ref[start : start + rows, :]
        for source, ref in tiles:
            value = jnp.where((block >= 0) & (block == source), ref[start : start + rows, :], value)
        return value

    ghost_y = jnp.where(grid.odd, select(2, Y_AT, ROWS), select(3, Y_AT, ROWS))
    ghost_z = jnp.where(grid.z >= 8, select(4, Z_AT, ROWS), select(5, Z_AT, ROWS))
    return ghost_y, ghost_z, select(0, X_HIGH_AT, 12), select(1, X_LOW_AT, 12)


def pull(grid, wet, own_ref, nb_ref, tiles, base_ref, work_ref, put):
    ghost_y, ghost_z, low_x, high_x = pick(grid, nb_ref, tiles, base_ref)
    ghost_x = {1: low_x, -1: high_x}
    wet_y = {
        1: lane_roll(ghost_y, 112 - 16 * WET_SLOT) > 0.5,
        -1: lane_roll(ghost_y, -16 * WET_SLOT) > 0.5,
    }
    wet_z = {
        1: lane_roll(ghost_z, 7 - WET_SLOT) > 0.5,
        -1: lane_roll(ghost_z, -WET_SLOT) > 0.5,
    }
    wet_x = {s: ghost_x[s][2 * WET_SLOT : 2 * WET_SLOT + 2, :] > 0.5 for s in (1, -1)}
    put(0, jnp.where(wet, own_ref[0], 0.0), None)
    for i in range(1, 19):
        c = VELOCITIES[i]
        a = own_ref[i]
        if c[0] != 0:
            j = outgoing(1 if c[0] > 0 else 0).index(i)
            at = 30 if c[0] > 0 else 0
            work_ref[i] = a
            work_ref[i, at : at + 2, :] = jnp.where(
                wet_x[c[0]], ghost_x[c[0]][2 * j : 2 * j + 2, :], BIG
            )
            a = work_ref[i]
        if c[1] != 0:
            j = outgoing(3 if c[1] > 0 else 2).index(i)
            ghost = lane_roll(ghost_y, 112 - 16 * j if c[1] > 0 else -16 * j)
            fine = wet_y[c[1]]
            if c[0] != 0:
                fine = fine & grid.beyond(1, c[1], 0, c[0])
            a = jnp.where(grid.plane(1, c[1]), jnp.where(fine, ghost, BIG), a)
        if c[2] != 0:
            j = outgoing(5 if c[2] > 0 else 4).index(i)
            ghost = lane_roll(ghost_z, 7 - j if c[2] > 0 else -j)
            fine = wet_z[c[2]]
            for other in (0, 1):
                if c[other] != 0:
                    fine = fine & grid.beyond(2, c[2], other, c[other])
            a = jnp.where(grid.plane(2, c[2]), jnp.where(fine, ghost, BIG), a)
        moved = flat_roll(grid, a, sum(c[d] * STRIDES[d] for d in range(3)))
        open_link = moved < LIMIT
        value = jnp.where(open_link, moved, own_ref[OPPOSITE[i]])
        put(i, jnp.where(wet, value, 0.0), open_link)


def first_kernel(pop_ref, fluid_ref, post_ref, pack_ref):
    grid = Grid()
    wet = fluid_ref[...] > 0
    g = collide([pop_ref[i] for i in range(19)], wet)
    for i in range(19):
        post_ref[i] = jnp.where(wet, g[i], BIG)
    write_pack(grid, g, wet, pack_ref)


def middle_kernel(own_ref, fluid_ref, nb_ref, p0, p1, p2, p3, post_ref, pack_ref, sum_hbm, work_ref, now_ref, sign_ref, sum_ref, sem):
    grid = Grid()
    wet = fluid_ref[...] > 0

    def put(i, value, open_link):
        now_ref[i] = value
        if i:
            sign_ref[i] = jnp.where(wet, jnp.where(open_link, 1.0, -1.0), 0.0)

    me = place()
    tiles = (
        (other_side(me), p0),
        (pair_mate(me), p1),
        (other_side(pair_mate(me)), p2),
        (pair_mate(other_side(me)), p3),
    )
    pull(grid, wet, own_ref, nb_ref, tiles, None, work_ref, put)
    g = collide([now_ref[i] for i in range(19)], wet)
    totals = [None] * 3
    for i in range(1, 19, 2):
        signed = (g[i] * sign_ref[i + 1] - g[i + 1] * sign_ref[i]) * WEIGHTS[i]
        for dim in range(3):
            c = VELOCITIES[i][dim]
            if c > 0:
                totals[dim] = signed if totals[dim] is None else totals[dim] + signed
            elif c < 0:
                totals[dim] = -signed if totals[dim] is None else totals[dim] - signed
    lane = lax.broadcasted_iota(jnp.int32, sum_ref.shape, 2)
    line = jnp.zeros(sum_ref.shape, jnp.float32)
    for dim in range(3):
        total = jnp.sum(jnp.sum(totals[dim], axis=0, keepdims=True), axis=1, keepdims=True)[None]
        line = jnp.where(lane == dim, total, line)
    sum_ref[...] = line
    sum_copy = pltpu.make_async_copy(sum_ref, sum_hbm, sem)
    sum_copy.start()
    for i in range(19):
        post_ref[i] = jnp.where(wet, g[i], BIG)
    write_pack(grid, g, wet, pack_ref)
    sum_copy.wait()


def pick_kernel(nb_ref, p0, p1, p3, tile_ref):
    me = place()
    tiles = ((other_side(me), p0), (pair_mate(me), p1), (pair_mate(other_side(me)), p3))
    ghost_y, ghost_z, low_x, high_x = pick(Grid(), nb_ref, tiles)
    tile_ref[Y_AT : Y_AT + ROWS, :] = ghost_y
    tile_ref[Z_AT : Z_AT + ROWS, :] = ghost_z
    tile_ref[X_HIGH_AT : X_HIGH_AT + 12, :] = low_x
    tile_ref[X_LOW_AT : X_LOW_AT + 12, :] = high_x


def last_kernel(own_ref, fluid_ref, nb_ref, base_ref, p2, out_ref, work_ref):
    grid = Grid()
    wet = fluid_ref[...] > 0

    def put(i, value, open_link):
        out_ref[i] = value

    pull(grid, wet, own_ref, nb_ref, ((other_side(pair_mate(place())), p2),), base_ref, work_ref, put)


def vmem(count):
    return [pl.BlockSpec(memory_space=pltpu.VMEM)] * count


def swap(pack, partner):
    length = lax.axis_size("node") * lax.axis_size("local")
    pairs = [(i, partner(i)) for i in range(length) if 0 <= partner(i) < length]
    return lax.ppermute(pack, ("node", "local"), pairs)


def exchange(pack):
    other = swap(pack, other_side)
    mate = swap(pack, pair_mate)
    return [other, mate]


def pass_on(other, mate):
    past_mate = swap(other, pair_mate)
    past_other = swap(mate, other_side)
    return [other, mate, past_mate, past_other]


def spread_out(lines, axis):
    return lax.all_to_all(lines, axis, 0, 0, tiled=True)


def shards(populations, fluid, neighbours):
    f32 = jnp.float32
    cube = jax.ShapeDtypeStruct((19, ROWS, LANES), f32)
    packed = jax.ShapeDtypeStruct((PACK_ROWS, LANES), f32)
    lines = jax.ShapeDtypeStruct((lax.axis_size("local"), 8, LANES), f32)
    scratch = pltpu.VMEM((19, ROWS, LANES), f32)
    smem = [pl.BlockSpec(memory_space=pltpu.SMEM)]
    devices = lax.axis_size("node") * lax.axis_size("local")
    params = pltpu.CompilerParams(vmem_limit_bytes=16 * 2**20)
    pop = populations.reshape(19, ROWS, LANES)
    wall = fluid.reshape(ROWS, LANES)

    post, pack = pl.pallas_call(
        first_kernel,
        out_shape=(cube, packed),
        in_specs=vmem(2),
        out_specs=tuple(vmem(2)),
        compiler_params=params,
        name="collide_first",
    )(pop, wall)
    ghosts = pass_on(*exchange(pack))
    post, pack, sums = pl.pallas_call(
        middle_kernel,
        out_shape=(cube, packed, lines),
        in_specs=vmem(2) + smem + vmem(4),
        out_specs=tuple(vmem(2)) + (pl.BlockSpec(memory_space=pl.ANY),),
        scratch_shapes=[scratch] * 3 + [pltpu.VMEM(lines.shape, f32), pltpu.SemaphoreType.DMA],
        compiler_params=params,
        name="stream_collide",
    )(post, wall, neighbours, *ghosts)
    sums = spread_out(sums, "local")
    other, mate = exchange(pack)
    sums, mate = lax.optimization_barrier((sums, mate))
    plane = jnp.sum(sums[:, 0, :], axis=0, keepdims=True)
    sums = spread_out(jnp.broadcast_to(plane, (lax.axis_size("node"), LANES)), "node")
    other, mate, past_mate, past_other = pass_on(other, mate)
    tile = pl.pallas_call(
        pick_kernel,
        out_shape=packed,
        in_specs=smem + vmem(3),
        out_specs=vmem(1)[0],
        compiler_params=params,
        name="pick_tiles",
        cost_estimate=pl.CostEstimate(flops=1000000, bytes_accessed=400000, transcendentals=0),
    )(neighbours, other, mate, past_other)
    out = pl.pallas_call(
        last_kernel,
        out_shape=cube,
        in_specs=vmem(2) + smem + vmem(2),
        out_specs=vmem(1)[0],
        scratch_shapes=[scratch],
        compiler_params=params,
        name="stream_last",
        cost_estimate=pl.CostEstimate(flops=4000000, bytes_accessed=1000000, transcendentals=0),
    )(post, wall, neighbours, tile, past_mate)
    flow = jnp.sum(sums, axis=0)[:3] / (devices * BLK * BLK)
    return out.reshape(populations.shape), flow


def solution(mesh):
    in_specs = (
        P(("node", "local"), None, None),
        P(("node", "local"), None),
        P(("node", "local"), None),
    )
    out_specs = (P(("node", "local"), None, None), P())
    return jax.shard_map(shards, mesh=mesh, in_specs=in_specs, out_specs=out_specs, check_vma=False)
```

```python
import functools

import jax
import jax.numpy as jnp
from jax import lax
from jax.experimental import pallas as pl
from jax.experimental.pallas import tpu as pltpu
from jax.sharding import PartitionSpec as P

BLK = 16
R = 2

VELOCITIES = (
    (0, 0, 0),
    (1, 0, 0),
    (-1, 0, 0),
    (0, 1, 0),
    (0, -1, 0),
    (0, 0, 1),
    (0, 0, -1),
    (1, 1, 0),
    (-1, -1, 0),
    (1, -1, 0),
    (-1, 1, 0),
    (1, 0, 1),
    (-1, 0, -1),
    (1, 0, -1),
    (-1, 0, 1),
    (0, 1, 1),
    (0, -1, -1),
    (0, 1, -1),
    (0, -1, 1),
)
WEIGHTS = (1.0 / 3.0,) + (1.0 / 18.0,) * 6 + (1.0 / 36.0,) * 12
OPPOSITE = (0, 2, 1, 4, 3, 6, 5, 8, 7, 10, 9, 12, 11, 14, 13, 16, 15, 18, 17)
OMEGA_PLUS = 1.6
MAGIC_PARAM = 0.1875
OMEGA_MINUS = 1.0 / (MAGIC_PARAM / (1.0 / OMEGA_PLUS - 0.5) + 0.5)
STRIDES = (256, 16, 1)

ROWS, LANES = 32, 128
PACK_ROWS = 88
Y_AT, Z_AT, X_LOW_AT, X_HIGH_AT = 0, 32, 64, 76
WET_SLOT = 5
BIG = 3.0e38
LIMIT = 1.0e38


def outgoing(face):
    sign = 1 if face % 2 else -1
    return [i for i in range(19) if VELOCITIES[i][face // 2] == sign]


class Grid:
    def __init__(self):
        self.row = lax.broadcasted_iota(jnp.int32, (ROWS, LANES), 0)
        self.lane = lax.broadcasted_iota(jnp.int32, (ROWS, LANES), 1)
        self.flat = self.row * LANES + self.lane
        self.odd = (self.row & 1) == 1
        self.z = self.lane & 15
        self.slot = self.lane >> 4

    def plane(self, dim, sign):
        if dim == 1:
            return self.odd & (self.slot == 7) if sign > 0 else (~self.odd) & (self.slot == 0)
        return self.z == (15 if sign > 0 else 0)

    def beyond(self, dim, sign, other, other_sign):
        source = (self.flat + sign * STRIDES[dim]) & 4095
        coord = source >> 8 if other == 0 else (source >> 4) & 15
        return coord != (15 if other_sign > 0 else 0)


def lane_roll(a, t):
    t %= LANES
    return a if t == 0 else pltpu.roll(a, t, 1)


def row_roll(a, q):
    q %= ROWS
    return a if q == 0 else pltpu.roll(a, q, 0)


def flat_roll(grid, a, shift):
    q, t = divmod(shift % 4096, LANES)
    if t == 0:
        return row_roll(a, q)
    rolled = lane_roll(a, t)
    return jnp.where(grid.lane >= t, row_roll(rolled, q), row_roll(rolled, q + 1))


def collide(g, wet):
    rho = g[0] * WEIGHTS[0]
    rho = rho + (g[1] + g[2] + g[3] + g[4] + g[5] + g[6]) * WEIGHTS[1]
    diagonal = g[7]
    for i in range(8, 19):
        diagonal = diagonal + g[i]
    rho = rho + diagonal * WEIGHTS[7]
    inverse = 1.0 / jnp.where(wet, rho, 1.0)
    u = []
    for dim in range(3):
        axis_part = diag_part = None
        for i in range(1, 19, 2):
            c = VELOCITIES[i][dim]
            if c == 0:
                continue
            diff = g[i] - g[i + 1] if c > 0 else g[i + 1] - g[i]
            if i < 7:
                axis_part = diff
            else:
                diag_part = diff if diag_part is None else diag_part + diff
        u.append((axis_part * WEIGHTS[1] + diag_part * WEIGHTS[7]) * inverse)
    speed_sq = u[0] * u[0] + u[1] * u[1] + u[2] * u[2]
    base = 1.0 - 1.5 * speed_sq
    out = [None] * 19
    out[0] = g[0] - (0.5 * OMEGA_PLUS) * (2.0 * g[0] - 2.0 * rho * base)
    for i in range(1, 19, 2):
        project = None
        for dim in range(3):
            c = VELOCITIES[i][dim]
            if c > 0:
                project = u[dim] if project is None else project + u[dim]
            elif c < 0:
                project = project - u[dim]
        even = (0.5 * OMEGA_PLUS) * ((g[i] + g[i + 1]) - 2.0 * rho * (base + 4.5 * project * project))
        odd = (0.5 * OMEGA_MINUS) * ((g[i] - g[i + 1]) - 6.0 * rho * project)
        out[i] = g[i] - even - odd
        out[i + 1] = g[i + 1] - even + odd
    return out


def write_pack(grid, g, wet, pack_ref):
    wet_value = jnp.where(wet, 1.0, 0.0)

    def of(face):
        return [g[i] for i in outgoing(face)] + [wet_value]

    low, high = of(2), of(3)
    pack = jnp.zeros((ROWS, LANES), jnp.float32)
    for j in range(6):
        both = jnp.where(grid.odd, lane_roll(high[j], 16 * (j + 1)), lane_roll(low[j], 16 * j))
        pack = jnp.where(grid.slot == j, both, pack)
    pack_ref[Y_AT : Y_AT + ROWS, :] = jnp.where(grid.odd, row_roll(pack, -2), row_roll(pack, 2))
    low, high = of(4), of(5)
    pack = jnp.zeros((ROWS, LANES), jnp.float32)
    for j in range(6):
        pack = jnp.where(grid.z == j, lane_roll(low[j], j), pack)
        pack = jnp.where(grid.z == 8 + j, lane_roll(high[j], j - 7), pack)
    pack_ref[Z_AT : Z_AT + ROWS, :] = jnp.where(
        grid.z >= 8, flat_roll(grid, pack, -16), flat_roll(grid, pack, 16)
    )
    low, high = of(0), of(1)
    for j in range(6):
        pack_ref[X_LOW_AT + 2 * j : X_LOW_AT + 2 * j + 2, :] = low[j][0:2, :]
        pack_ref[X_HIGH_AT + 2 * j : X_HIGH_AT + 2 * j + 2, :] = high[j][30:32, :]


def pair_mate(me):
    return me ^ 1


def other_side(me):
    return ((me + 1) ^ 1) - 1


def place():
    return lax.axis_index("node") * lax.axis_size("local") + lax.axis_index("local")


def pick(grid, nb_ref, tiles, base_ref=None):
    def select(face, start, rows):
        block = nb_ref[0, face]
        if base_ref is None:
            value = jnp.zeros((rows, LANES), jnp.float32)
        else:
            value = base_ref[start : start + rows, :]
        for source, ref in tiles:
            value = jnp.where((block >= 0) & (block == source), ref[start : start + rows, :], value)
        return value

    ghost_y = jnp.where(grid.odd, select(2, Y_AT, ROWS), select(3, Y_AT, ROWS))
    ghost_z = jnp.where(grid.z >= 8, select(4, Z_AT, ROWS), select(5, Z_AT, ROWS))
    return ghost_y, ghost_z, select(0, X_HIGH_AT, 12), select(1, X_LOW_AT, 12)


def pull(grid, wet, own_ref, nb_ref, tiles, base_ref, work_ref, put):
    ghost_y, ghost_z, low_x, high_x = pick(grid, nb_ref, tiles, base_ref)
    ghost_x = {1: low_x, -1: high_x}
    wet_y = {
        1: lane_roll(ghost_y, 112 - 16 * WET_SLOT) > 0.5,
        -1: lane_roll(ghost_y, -16 * WET_SLOT) > 0.5,
    }
    wet_z = {
        1: lane_roll(ghost_z, 7 - WET_SLOT) > 0.5,
        -1: lane_roll(ghost_z, -WET_SLOT) > 0.5,
    }
    wet_x = {s: ghost_x[s][2 * WET_SLOT : 2 * WET_SLOT + 2, :] > 0.5 for s in (1, -1)}
    put(0, jnp.where(wet, own_ref[0], 0.0), None)
    for i in range(1, 19):
        c = VELOCITIES[i]
        a = own_ref[i]
        if c[0] != 0:
            j = outgoing(1 if c[0] > 0 else 0).index(i)
            at = 30 if c[0] > 0 else 0
            work_ref[i] = a
            work_ref[i, at : at + 2, :] = jnp.where(
                wet_x[c[0]], ghost_x[c[0]][2 * j : 2 * j + 2, :], BIG
            )
            a = work_ref[i]
        if c[1] != 0:
            j = outgoing(3 if c[1] > 0 else 2).index(i)
            ghost = lane_roll(ghost_y, 112 - 16 * j if c[1] > 0 else -16 * j)
            fine = wet_y[c[1]]
            if c[0] != 0:
                fine = fine & grid.beyond(1, c[1], 0, c[0])
            a = jnp.where(grid.plane(1, c[1]), jnp.where(fine, ghost, BIG), a)
        if c[2] != 0:
            j = outgoing(5 if c[2] > 0 else 4).index(i)
            ghost = lane_roll(ghost_z, 7 - j if c[2] > 0 else -j)
            fine = wet_z[c[2]]
            for other in (0, 1):
                if c[other] != 0:
                    fine = fine & grid.beyond(2, c[2], other, c[other])
            a = jnp.where(grid.plane(2, c[2]), jnp.where(fine, ghost, BIG), a)
        moved = flat_roll(grid, a, sum(c[d] * STRIDES[d] for d in range(3)))
        open_link = moved < LIMIT
        value = jnp.where(open_link, moved, own_ref[OPPOSITE[i]])
        put(i, jnp.where(wet, value, 0.0), open_link)


def first_kernel(pop_ref, fluid_ref, post_ref, pack_ref):
    grid = Grid()
    wet = fluid_ref[...] > 0
    g = collide([pop_ref[i] for i in range(19)], wet)
    for i in range(19):
        post_ref[i] = jnp.where(wet, g[i], BIG)
    write_pack(grid, g, wet, pack_ref)


def middle_kernel(own_ref, fluid_ref, nb_ref, p0, p1, p2, p3, post_ref, pack_ref, sum_hbm, work_ref, now_ref, sign_ref, sum_ref, sem):
    grid = Grid()
    wet = fluid_ref[...] > 0

    def put(i, value, open_link):
        now_ref[i] = value
        if i:
            sign_ref[i] = jnp.where(wet, jnp.where(open_link, 1.0, -1.0), 0.0)

    me = place()
    tiles = (
        (other_side(me), p0),
        (pair_mate(me), p1),
        (other_side(pair_mate(me)), p2),
        (pair_mate(other_side(me)), p3),
    )
    pull(grid, wet, own_ref, nb_ref, tiles, None, work_ref, put)
    g = collide([now_ref[i] for i in range(19)], wet)
    totals = [None] * 3
    for i in range(1, 19, 2):
        signed = (g[i] * sign_ref[i + 1] - g[i + 1] * sign_ref[i]) * WEIGHTS[i]
        for dim in range(3):
            c = VELOCITIES[i][dim]
            if c > 0:
                totals[dim] = signed if totals[dim] is None else totals[dim] + signed
            elif c < 0:
                totals[dim] = -signed if totals[dim] is None else totals[dim] - signed
    lane = lax.broadcasted_iota(jnp.int32, sum_ref.shape, 2)
    line = jnp.zeros(sum_ref.shape, jnp.float32)
    for dim in range(3):
        total = jnp.sum(jnp.sum(totals[dim], axis=0, keepdims=True), axis=1, keepdims=True)[None]
        line = jnp.where(lane == dim, total, line)
    sum_ref[...] = line
    sum_copy = pltpu.make_async_copy(sum_ref, sum_hbm, sem)
    sum_copy.start()
    for i in range(19):
        post_ref[i] = jnp.where(wet, g[i], BIG)
    write_pack(grid, g, wet, pack_ref)
    sum_copy.wait()


def pick_kernel(nb_ref, p0, p1, p3, tile_ref):
    me = place()
    tiles = ((other_side(me), p0), (pair_mate(me), p1), (pair_mate(other_side(me)), p3))
    ghost_y, ghost_z, low_x, high_x = pick(Grid(), nb_ref, tiles)
    tile_ref[Y_AT : Y_AT + ROWS, :] = ghost_y
    tile_ref[Z_AT : Z_AT + ROWS, :] = ghost_z
    tile_ref[X_HIGH_AT : X_HIGH_AT + 12, :] = low_x
    tile_ref[X_LOW_AT : X_LOW_AT + 12, :] = high_x


def last_kernel(own_ref, fluid_ref, nb_ref, base_ref, p2, out_ref, work_ref):
    grid = Grid()
    wet = fluid_ref[...] > 0

    def put(i, value, open_link):
        out_ref[i] = value

    pull(grid, wet, own_ref, nb_ref, ((other_side(pair_mate(place())), p2),), base_ref, work_ref, put)


def vmem(count):
    return [pl.BlockSpec(memory_space=pltpu.VMEM)] * count


def swap(pack, partner):
    length = lax.axis_size("node") * lax.axis_size("local")
    pairs = [(i, partner(i)) for i in range(length) if 0 <= partner(i) < length]
    return lax.ppermute(pack, ("node", "local"), pairs)


def exchange(pack):
    other = swap(pack, other_side)
    mate = swap(pack, pair_mate)
    return [other, mate]


def pass_on(other, mate):
    past_mate = swap(other, pair_mate)
    past_other = swap(mate, other_side)
    return [other, mate, past_mate, past_other]


CORES = 2


def spread_out(lines, groups):
    return lax.all_to_all(lines, ("node", "local"), 0, 0, tiled=True, axis_index_groups=groups)


def shards(populations, fluid, neighbours):
    f32 = jnp.float32
    cube = jax.ShapeDtypeStruct((19, ROWS, LANES), f32)
    packed = jax.ShapeDtypeStruct((PACK_ROWS, LANES), f32)
    layer = CORES * lax.axis_size("local")
    layers = lax.axis_size("node") // CORES
    in_layer = [[z * layer + i for i in range(layer)] for z in range(layers)]
    across_layers = [[z * layer + i for z in range(layers)] for i in range(layer)]
    lines = jax.ShapeDtypeStruct((layer, 4, LANES), f32)
    scratch = pltpu.VMEM((19, ROWS, LANES), f32)
    smem = [pl.BlockSpec(memory_space=pltpu.SMEM)]
    devices = lax.axis_size("node") * lax.axis_size("local")
    params = pltpu.CompilerParams(vmem_limit_bytes=16 * 2**20)
    pop = populations.reshape(19, ROWS, LANES)
    wall = fluid.reshape(ROWS, LANES)

    post, pack = pl.pallas_call(
        first_kernel,
        out_shape=(cube, packed),
        in_specs=vmem(2),
        out_specs=tuple(vmem(2)),
        compiler_params=params,
        name="collide_first",
    )(pop, wall)
    ghosts = pass_on(*exchange(pack))
    post, pack, sums = pl.pallas_call(
        middle_kernel,
        out_shape=(cube, packed, lines),
        in_specs=vmem(2) + smem + vmem(4),
        out_specs=tuple(vmem(2)) + (pl.BlockSpec(memory_space=pl.ANY),),
        scratch_shapes=[scratch] * 3 + [pltpu.VMEM(lines.shape, f32), pltpu.SemaphoreType.DMA],
        compiler_params=params,
        name="stream_collide",
    )(post, wall, neighbours, *ghosts)
    sums = spread_out(sums, in_layer)
    other, mate = exchange(pack)
    sums, mate = lax.optimization_barrier((sums, mate))
    plane = jnp.sum(sums[:, 0, :], axis=0)[None, None]
    sums = spread_out(jnp.broadcast_to(plane, (layers, 4, LANES)), across_layers)
    other, mate, past_mate, past_other = pass_on(other, mate)
    tile = pl.pallas_call(
        pick_kernel,
        out_shape=packed,
        in_specs=smem + vmem(3),
        out_specs=vmem(1)[0],
        compiler_params=params,
        name="pick_tiles",
        cost_estimate=pl.CostEstimate(flops=1000000, bytes_accessed=400000, transcendentals=0),
    )(neighbours, other, mate, past_other)
    out = pl.pallas_call(
        last_kernel,
        out_shape=cube,
        in_specs=vmem(2) + smem + vmem(2),
        out_specs=vmem(1)[0],
        scratch_shapes=[scratch],
        compiler_params=params,
        name="stream_last",
        cost_estimate=pl.CostEstimate(flops=4000000, bytes_accessed=1000000, transcendentals=0),
    )(post, wall, neighbours, tile, past_mate)
    flow = jnp.sum(sums[:, 0, :3], axis=0) / (devices * BLK * BLK)
    return out.reshape(populations.shape), flow


def solution(mesh):
    in_specs = (
        P(("node", "local"), None, None),
        P(("node", "local"), None),
        P(("node", "local"), None),
    )
    out_specs = (P(("node", "local"), None, None), P())
    return jax.shard_map(shards, mesh=mesh, in_specs=in_specs, out_specs=out_specs, check_vma=False)
```

```python
import functools

import jax
import jax.numpy as jnp
from jax import lax
from jax.experimental import pallas as pl
from jax.experimental.pallas import tpu as pltpu
from jax.sharding import PartitionSpec as P

BLK = 16
R = 2

VELOCITIES = (
    (0, 0, 0),
    (1, 0, 0),
    (-1, 0, 0),
    (0, 1, 0),
    (0, -1, 0),
    (0, 0, 1),
    (0, 0, -1),
    (1, 1, 0),
    (-1, -1, 0),
    (1, -1, 0),
    (-1, 1, 0),
    (1, 0, 1),
    (-1, 0, -1),
    (1, 0, -1),
    (-1, 0, 1),
    (0, 1, 1),
    (0, -1, -1),
    (0, 1, -1),
    (0, -1, 1),
)
WEIGHTS = (1.0 / 3.0,) + (1.0 / 18.0,) * 6 + (1.0 / 36.0,) * 12
OPPOSITE = (0, 2, 1, 4, 3, 6, 5, 8, 7, 10, 9, 12, 11, 14, 13, 16, 15, 18, 17)
OMEGA_PLUS = 1.6
MAGIC_PARAM = 0.1875
OMEGA_MINUS = 1.0 / (MAGIC_PARAM / (1.0 / OMEGA_PLUS - 0.5) + 0.5)
STRIDES = (256, 16, 1)

ROWS, LANES = 32, 128
PACK_ROWS = 88
Y_AT, Z_AT, X_LOW_AT, X_HIGH_AT = 0, 32, 64, 76
WET_SLOT = 5
BIG = 3.0e38
LIMIT = 1.0e38


def outgoing(face):
    sign = 1 if face % 2 else -1
    return [i for i in range(19) if VELOCITIES[i][face // 2] == sign]


class Grid:
    def __init__(self):
        self.row = lax.broadcasted_iota(jnp.int32, (ROWS, LANES), 0)
        self.lane = lax.broadcasted_iota(jnp.int32, (ROWS, LANES), 1)
        self.flat = self.row * LANES + self.lane
        self.odd = (self.row & 1) == 1
        self.z = self.lane & 15
        self.slot = self.lane >> 4

    def plane(self, dim, sign):
        if dim == 1:
            return self.odd & (self.slot == 7) if sign > 0 else (~self.odd) & (self.slot == 0)
        return self.z == (15 if sign > 0 else 0)

    def beyond(self, dim, sign, other, other_sign):
        source = (self.flat + sign * STRIDES[dim]) & 4095
        coord = source >> 8 if other == 0 else (source >> 4) & 15
        return coord != (15 if other_sign > 0 else 0)


def lane_roll(a, t):
    t %= LANES
    return a if t == 0 else pltpu.roll(a, t, 1)


def row_roll(a, q):
    q %= ROWS
    return a if q == 0 else pltpu.roll(a, q, 0)


def flat_roll(grid, a, shift):
    q, t = divmod(shift % 4096, LANES)
    if t == 0:
        return row_roll(a, q)
    rolled = lane_roll(a, t)
    return jnp.where(grid.lane >= t, row_roll(rolled, q), row_roll(rolled, q + 1))


def collide(g, wet):
    rho = g[0] * WEIGHTS[0]
    rho = rho + (g[1] + g[2] + g[3] + g[4] + g[5] + g[6]) * WEIGHTS[1]
    diagonal = g[7]
    for i in range(8, 19):
        diagonal = diagonal + g[i]
    rho = rho + diagonal * WEIGHTS[7]
    inverse = 1.0 / jnp.where(wet, rho, 1.0)
    u = []
    for dim in range(3):
        axis_part = diag_part = None
        for i in range(1, 19, 2):
            c = VELOCITIES[i][dim]
            if c == 0:
                continue
            diff = g[i] - g[i + 1] if c > 0 else g[i + 1] - g[i]
            if i < 7:
                axis_part = diff
            else:
                diag_part = diff if diag_part is None else diag_part + diff
        u.append((axis_part * WEIGHTS[1] + diag_part * WEIGHTS[7]) * inverse)
    speed_sq = u[0] * u[0] + u[1] * u[1] + u[2] * u[2]
    base = 1.0 - 1.5 * speed_sq
    out = [None] * 19
    out[0] = g[0] - (0.5 * OMEGA_PLUS) * (2.0 * g[0] - 2.0 * rho * base)
    for i in range(1, 19, 2):
        project = None
        for dim in range(3):
            c = VELOCITIES[i][dim]
            if c > 0:
                project = u[dim] if project is None else project + u[dim]
            elif c < 0:
                project = project - u[dim]
        even = (0.5 * OMEGA_PLUS) * ((g[i] + g[i + 1]) - 2.0 * rho * (base + 4.5 * project * project))
        odd = (0.5 * OMEGA_MINUS) * ((g[i] - g[i + 1]) - 6.0 * rho * project)
        out[i] = g[i] - even - odd
        out[i + 1] = g[i + 1] - even + odd
    return out


def write_pack(grid, g, wet, pack_ref):
    wet_value = jnp.where(wet, 1.0, 0.0)

    def of(face):
        return [g[i] for i in outgoing(face)] + [wet_value]

    low, high = of(2), of(3)
    pack = jnp.zeros((ROWS, LANES), jnp.float32)
    for j in range(6):
        both = jnp.where(grid.odd, lane_roll(high[j], 16 * (j + 1)), lane_roll(low[j], 16 * j))
        pack = jnp.where(grid.slot == j, both, pack)
    pack_ref[Y_AT : Y_AT + ROWS, :] = jnp.where(grid.odd, row_roll(pack, -2), row_roll(pack, 2))
    low, high = of(4), of(5)
    pack = jnp.zeros((ROWS, LANES), jnp.float32)
    for j in range(6):
        pack = jnp.where(grid.z == j, lane_roll(low[j], j), pack)
        pack = jnp.where(grid.z == 8 + j, lane_roll(high[j], j - 7), pack)
    pack_ref[Z_AT : Z_AT + ROWS, :] = jnp.where(
        grid.z >= 8, flat_roll(grid, pack, -16), flat_roll(grid, pack, 16)
    )
    low, high = of(0), of(1)
    for j in range(6):
        pack_ref[X_LOW_AT + 2 * j : X_LOW_AT + 2 * j + 2, :] = low[j][0:2, :]
        pack_ref[X_HIGH_AT + 2 * j : X_HIGH_AT + 2 * j + 2, :] = high[j][30:32, :]


def pair_mate(me):
    return me ^ 1


def other_side(me):
    return ((me + 1) ^ 1) - 1


def place():
    return lax.axis_index("node") * lax.axis_size("local") + lax.axis_index("local")


def pick(grid, nb_ref, tiles, base_ref=None):
    def select(face, start, rows):
        block = nb_ref[0, face]
        if base_ref is None:
            value = jnp.zeros((rows, LANES), jnp.float32)
        else:
            value = base_ref[start : start + rows, :]
        for source, ref in tiles:
            value = jnp.where((block >= 0) & (block == source), ref[start : start + rows, :], value)
        return value

    ghost_y = jnp.where(grid.odd, select(2, Y_AT, ROWS), select(3, Y_AT, ROWS))
    ghost_z = jnp.where(grid.z >= 8, select(4, Z_AT, ROWS), select(5, Z_AT, ROWS))
    return ghost_y, ghost_z, select(0, X_HIGH_AT, 12), select(1, X_LOW_AT, 12)


def pull(grid, wet, own_ref, nb_ref, tiles, base_ref, work_ref, put):
    ghost_y, ghost_z, low_x, high_x = pick(grid, nb_ref, tiles, base_ref)
    ghost_x = {1: low_x, -1: high_x}
    wet_y = {
        1: lane_roll(ghost_y, 112 - 16 * WET_SLOT) > 0.5,
        -1: lane_roll(ghost_y, -16 * WET_SLOT) > 0.5,
    }
    wet_z = {
        1: lane_roll(ghost_z, 7 - WET_SLOT) > 0.5,
        -1: lane_roll(ghost_z, -WET_SLOT) > 0.5,
    }
    wet_x = {s: ghost_x[s][2 * WET_SLOT : 2 * WET_SLOT + 2, :] > 0.5 for s in (1, -1)}
    put(0, jnp.where(wet, own_ref[0], 0.0), None)
    for i in range(1, 19):
        c = VELOCITIES[i]
        a = own_ref[i]
        if c[0] != 0:
            j = outgoing(1 if c[0] > 0 else 0).index(i)
            at = 30 if c[0] > 0 else 0
            work_ref[i] = a
            work_ref[i, at : at + 2, :] = jnp.where(
                wet_x[c[0]], ghost_x[c[0]][2 * j : 2 * j + 2, :], BIG
            )
            a = work_ref[i]
        if c[1] != 0:
            j = outgoing(3 if c[1] > 0 else 2).index(i)
            ghost = lane_roll(ghost_y, 112 - 16 * j if c[1] > 0 else -16 * j)
            fine = wet_y[c[1]]
            if c[0] != 0:
                fine = fine & grid.beyond(1, c[1], 0, c[0])
            a = jnp.where(grid.plane(1, c[1]), jnp.where(fine, ghost, BIG), a)
        if c[2] != 0:
            j = outgoing(5 if c[2] > 0 else 4).index(i)
            ghost = lane_roll(ghost_z, 7 - j if c[2] > 0 else -j)
            fine = wet_z[c[2]]
            for other in (0, 1):
                if c[other] != 0:
                    fine = fine & grid.beyond(2, c[2], other, c[other])
            a = jnp.where(grid.plane(2, c[2]), jnp.where(fine, ghost, BIG), a)
        moved = flat_roll(grid, a, sum(c[d] * STRIDES[d] for d in range(3)))
        open_link = moved < LIMIT
        value = jnp.where(open_link, moved, own_ref[OPPOSITE[i]])
        put(i, jnp.where(wet, value, 0.0), open_link)


def first_kernel(pop_ref, fluid_ref, post_ref, pack_ref):
    grid = Grid()
    wet = fluid_ref[...] > 0
    g = collide([pop_ref[i] for i in range(19)], wet)
    for i in range(19):
        post_ref[i] = jnp.where(wet, g[i], BIG)
    write_pack(grid, g, wet, pack_ref)


def middle_kernel(own_ref, fluid_ref, nb_ref, p0, p1, p2, p3, post_ref, pack_ref, sum_hbm, work_ref, now_ref, sign_ref, sum_ref, sem):
    grid = Grid()
    wet = fluid_ref[...] > 0

    def put(i, value, open_link):
        now_ref[i] = value
        if i:
            sign_ref[i] = jnp.where(wet, jnp.where(open_link, 1.0, -1.0), 0.0)

    me = place()
    tiles = (
        (other_side(me), p0),
        (pair_mate(me), p1),
        (other_side(pair_mate(me)), p2),
        (pair_mate(other_side(me)), p3),
    )
    pull(grid, wet, own_ref, nb_ref, tiles, None, work_ref, put)
    g = collide([now_ref[i] for i in range(19)], wet)
    totals = [None] * 3
    for i in range(1, 19, 2):
        signed = (g[i] * sign_ref[i + 1] - g[i + 1] * sign_ref[i]) * WEIGHTS[i]
        for dim in range(3):
            c = VELOCITIES[i][dim]
            if c > 0:
                totals[dim] = signed if totals[dim] is None else totals[dim] + signed
            elif c < 0:
                totals[dim] = -signed if totals[dim] is None else totals[dim] - signed
    lane = lax.broadcasted_iota(jnp.int32, sum_ref.shape, 2)
    line = jnp.zeros(sum_ref.shape, jnp.float32)
    for dim in range(3):
        total = jnp.sum(jnp.sum(totals[dim], axis=0, keepdims=True), axis=1, keepdims=True)[None]
        line = jnp.where(lane == dim, total, line)
    sum_ref[...] = line
    sum_copy = pltpu.make_async_copy(sum_ref, sum_hbm, sem)
    sum_copy.start()
    for i in range(19):
        post_ref[i] = jnp.where(wet, g[i], BIG)
    write_pack(grid, g, wet, pack_ref)
    sum_copy.wait()


def pick_kernel(nb_ref, p0, p1, p3, tile_ref):
    me = place()
    tiles = ((other_side(me), p0), (pair_mate(me), p1), (pair_mate(other_side(me)), p3))
    ghost_y, ghost_z, low_x, high_x = pick(Grid(), nb_ref, tiles)
    tile_ref[Y_AT : Y_AT + ROWS, :] = ghost_y
    tile_ref[Z_AT : Z_AT + ROWS, :] = ghost_z
    tile_ref[X_HIGH_AT : X_HIGH_AT + 12, :] = low_x
    tile_ref[X_LOW_AT : X_LOW_AT + 12, :] = high_x


def last_kernel(own_ref, fluid_ref, nb_ref, base_ref, p2, out_ref, work_ref):
    grid = Grid()
    wet = fluid_ref[...] > 0

    def put(i, value, open_link):
        out_ref[i] = value

    pull(grid, wet, own_ref, nb_ref, ((other_side(pair_mate(place())), p2),), base_ref, work_ref, put)


def vmem(count):
    return [pl.BlockSpec(memory_space=pltpu.VMEM)] * count


def swap(pack, partner):
    length = lax.axis_size("node") * lax.axis_size("local")
    pairs = [(i, partner(i)) for i in range(length) if 0 <= partner(i) < length]
    return lax.ppermute(pack, ("node", "local"), pairs)


def exchange(pack):
    other = swap(pack, other_side)
    mate = swap(pack, pair_mate)
    return [other, mate]


def pass_on(other, mate):
    past_mate = swap(other, pair_mate)
    past_other = swap(mate, other_side)
    return [other, mate, past_mate, past_other]


CORES = 2


def spread_out(lines, groups):
    return lax.all_to_all(lines, ("node", "local"), 0, 0, tiled=True, axis_index_groups=groups)


def shards(populations, fluid, neighbours):
    f32 = jnp.float32
    cube = jax.ShapeDtypeStruct((19, ROWS, LANES), f32)
    packed = jax.ShapeDtypeStruct((PACK_ROWS, LANES), f32)
    layer = CORES * lax.axis_size("local")
    layers = lax.axis_size("node") // CORES
    in_layer = [[z * layer + i for i in range(layer)] for z in range(layers)]
    across_layers = [[z * layer + i for z in range(layers)] for i in range(layer)]
    lines = jax.ShapeDtypeStruct((layer, 4, LANES), f32)
    scratch = pltpu.VMEM((19, ROWS, LANES), f32)
    smem = [pl.BlockSpec(memory_space=pltpu.SMEM)]
    devices = lax.axis_size("node") * lax.axis_size("local")
    params = pltpu.CompilerParams(vmem_limit_bytes=16 * 2**20)
    pop = populations.reshape(19, ROWS, LANES)
    wall = fluid.reshape(ROWS, LANES)

    post, pack = pl.pallas_call(
        first_kernel,
        out_shape=(cube, packed),
        in_specs=vmem(2),
        out_specs=tuple(vmem(2)),
        compiler_params=params,
        name="collide_first",
    )(pop, wall)
    ghosts = pass_on(*exchange(pack))
    post, pack, sums = pl.pallas_call(
        middle_kernel,
        out_shape=(cube, packed, lines),
        in_specs=vmem(2) + smem + vmem(4),
        out_specs=tuple(vmem(2)) + (pl.BlockSpec(memory_space=pl.ANY),),
        scratch_shapes=[scratch] * 3 + [pltpu.VMEM(lines.shape, f32), pltpu.SemaphoreType.DMA],
        compiler_params=params,
        name="stream_collide",
    )(post, wall, neighbours, *ghosts)
    sums = spread_out(sums, in_layer)
    other, mate = exchange(pack)
    sums, mate = lax.optimization_barrier((sums, mate))
    plane = jnp.sum(sums[:, 0, :], axis=0)[None, None]
    sums = spread_out(jnp.broadcast_to(plane, (layers, 2, LANES)), across_layers)
    other, mate, past_mate, past_other = pass_on(other, mate)
    tile = pl.pallas_call(
        pick_kernel,
        out_shape=packed,
        in_specs=smem + vmem(3),
        out_specs=vmem(1)[0],
        compiler_params=params,
        name="pick_tiles",
        cost_estimate=pl.CostEstimate(flops=1000000, bytes_accessed=400000, transcendentals=0),
    )(neighbours, other, mate, past_other)
    out = pl.pallas_call(
        last_kernel,
        out_shape=cube,
        in_specs=vmem(2) + smem + vmem(2),
        out_specs=vmem(1)[0],
        scratch_shapes=[scratch],
        compiler_params=params,
        name="stream_last",
        cost_estimate=pl.CostEstimate(flops=4000000, bytes_accessed=1000000, transcendentals=0),
    )(post, wall, neighbours, tile, past_mate)
    flow = jnp.sum(sums[:, 0, :3], axis=0) / (devices * BLK * BLK)
    return out.reshape(populations.shape), flow


def solution(mesh):
    in_specs = (
        P(("node", "local"), None, None),
        P(("node", "local"), None),
        P(("node", "local"), None),
    )
    out_specs = (P(("node", "local"), None, None), P())
    return jax.shard_map(shards, mesh=mesh, in_specs=in_specs, out_specs=out_specs, check_vma=False)
```

```python
import functools

import jax
import jax.numpy as jnp
from jax import lax
from jax.experimental import pallas as pl
from jax.experimental.pallas import tpu as pltpu
from jax.sharding import PartitionSpec as P

BLK = 16
R = 2

VELOCITIES = (
    (0, 0, 0),
    (1, 0, 0),
    (-1, 0, 0),
    (0, 1, 0),
    (0, -1, 0),
    (0, 0, 1),
    (0, 0, -1),
    (1, 1, 0),
    (-1, -1, 0),
    (1, -1, 0),
    (-1, 1, 0),
    (1, 0, 1),
    (-1, 0, -1),
    (1, 0, -1),
    (-1, 0, 1),
    (0, 1, 1),
    (0, -1, -1),
    (0, 1, -1),
    (0, -1, 1),
)
WEIGHTS = (1.0 / 3.0,) + (1.0 / 18.0,) * 6 + (1.0 / 36.0,) * 12
OPPOSITE = (0, 2, 1, 4, 3, 6, 5, 8, 7, 10, 9, 12, 11, 14, 13, 16, 15, 18, 17)
OMEGA_PLUS = 1.6
MAGIC_PARAM = 0.1875
OMEGA_MINUS = 1.0 / (MAGIC_PARAM / (1.0 / OMEGA_PLUS - 0.5) + 0.5)
STRIDES = (256, 16, 1)

ROWS, LANES = 32, 128
PACK_ROWS = 88
Y_AT, Z_AT, X_LOW_AT, X_HIGH_AT = 0, 32, 64, 76
WET_SLOT = 5
BIG = 3.0e38
LIMIT = 1.0e38


def outgoing(face):
    sign = 1 if face % 2 else -1
    return [i for i in range(19) if VELOCITIES[i][face // 2] == sign]


class Grid:
    def __init__(self):
        self.row = lax.broadcasted_iota(jnp.int32, (ROWS, LANES), 0)
        self.lane = lax.broadcasted_iota(jnp.int32, (ROWS, LANES), 1)
        self.flat = self.row * LANES + self.lane
        self.odd = (self.row & 1) == 1
        self.z = self.lane & 15
        self.slot = self.lane >> 4

    def plane(self, dim, sign):
        if dim == 1:
            return self.odd & (self.slot == 7) if sign > 0 else (~self.odd) & (self.slot == 0)
        return self.z == (15 if sign > 0 else 0)

    def beyond(self, dim, sign, other, other_sign):
        source = (self.flat + sign * STRIDES[dim]) & 4095
        coord = source >> 8 if other == 0 else (source >> 4) & 15
        return coord != (15 if other_sign > 0 else 0)


def lane_roll(a, t):
    t %= LANES
    return a if t == 0 else pltpu.roll(a, t, 1)


def row_roll(a, q):
    q %= ROWS
    return a if q == 0 else pltpu.roll(a, q, 0)


def flat_roll(grid, a, shift):
    q, t = divmod(shift % 4096, LANES)
    if t == 0:
        return row_roll(a, q)
    rolled = lane_roll(a, t)
    return jnp.where(grid.lane >= t, row_roll(rolled, q), row_roll(rolled, q + 1))


def collide(g, wet):
    rho = g[0] * WEIGHTS[0]
    rho = rho + (g[1] + g[2] + g[3] + g[4] + g[5] + g[6]) * WEIGHTS[1]
    diagonal = g[7]
    for i in range(8, 19):
        diagonal = diagonal + g[i]
    rho = rho + diagonal * WEIGHTS[7]
    inverse = 1.0 / jnp.where(wet, rho, 1.0)
    u = []
    for dim in range(3):
        axis_part = diag_part = None
        for i in range(1, 19, 2):
            c = VELOCITIES[i][dim]
            if c == 0:
                continue
            diff = g[i] - g[i + 1] if c > 0 else g[i + 1] - g[i]
            if i < 7:
                axis_part = diff
            else:
                diag_part = diff if diag_part is None else diag_part + diff
        u.append((axis_part * WEIGHTS[1] + diag_part * WEIGHTS[7]) * inverse)
    speed_sq = u[0] * u[0] + u[1] * u[1] + u[2] * u[2]
    base = 1.0 - 1.5 * speed_sq
    out = [None] * 19
    out[0] = g[0] - (0.5 * OMEGA_PLUS) * (2.0 * g[0] - 2.0 * rho * base)
    for i in range(1, 19, 2):
        project = None
        for dim in range(3):
            c = VELOCITIES[i][dim]
            if c > 0:
                project = u[dim] if project is None else project + u[dim]
            elif c < 0:
                project = project - u[dim]
        even = (0.5 * OMEGA_PLUS) * ((g[i] + g[i + 1]) - 2.0 * rho * (base + 4.5 * project * project))
        odd = (0.5 * OMEGA_MINUS) * ((g[i] - g[i + 1]) - 6.0 * rho * project)
        out[i] = g[i] - even - odd
        out[i + 1] = g[i + 1] - even + odd
    return out


def write_pack(grid, g, wet, pack_ref):
    wet_value = jnp.where(wet, 1.0, 0.0)

    def of(face):
        return [g[i] for i in outgoing(face)] + [wet_value]

    low, high = of(2), of(3)
    pack = jnp.zeros((ROWS, LANES), jnp.float32)
    for j in range(6):
        both = jnp.where(grid.odd, lane_roll(high[j], 16 * (j + 1)), lane_roll(low[j], 16 * j))
        pack = jnp.where(grid.slot == j, both, pack)
    pack_ref[Y_AT : Y_AT + ROWS, :] = jnp.where(grid.odd, row_roll(pack, -2), row_roll(pack, 2))
    low, high = of(4), of(5)
    pack = jnp.zeros((ROWS, LANES), jnp.float32)
    for j in range(6):
        pack = jnp.where(grid.z == j, lane_roll(low[j], j), pack)
        pack = jnp.where(grid.z == 8 + j, lane_roll(high[j], j - 7), pack)
    pack_ref[Z_AT : Z_AT + ROWS, :] = jnp.where(
        grid.z >= 8, flat_roll(grid, pack, -16), flat_roll(grid, pack, 16)
    )
    low, high = of(0), of(1)
    for j in range(6):
        pack_ref[X_LOW_AT + 2 * j : X_LOW_AT + 2 * j + 2, :] = low[j][0:2, :]
        pack_ref[X_HIGH_AT + 2 * j : X_HIGH_AT + 2 * j + 2, :] = high[j][30:32, :]


def pair_mate(me):
    return me ^ 1


def other_side(me):
    return ((me + 1) ^ 1) - 1


def place():
    return lax.axis_index("node") * lax.axis_size("local") + lax.axis_index("local")


def pick(grid, nb_ref, tiles, base_ref=None):
    def select(face, start, rows):
        block = nb_ref[0, face]
        if base_ref is None:
            value = jnp.zeros((rows, LANES), jnp.float32)
        else:
            value = base_ref[start : start + rows, :]
        for source, ref in tiles:
            value = jnp.where((block >= 0) & (block == source), ref[start : start + rows, :], value)
        return value

    ghost_y = jnp.where(grid.odd, select(2, Y_AT, ROWS), select(3, Y_AT, ROWS))
    ghost_z = jnp.where(grid.z >= 8, select(4, Z_AT, ROWS), select(5, Z_AT, ROWS))
    return ghost_y, ghost_z, select(0, X_HIGH_AT, 12), select(1, X_LOW_AT, 12)


def pull(grid, wet, own_ref, nb_ref, tiles, base_ref, work_ref, put):
    ghost_y, ghost_z, low_x, high_x = pick(grid, nb_ref, tiles, base_ref)
    ghost_x = {1: low_x, -1: high_x}
    wet_y = {
        1: lane_roll(ghost_y, 112 - 16 * WET_SLOT) > 0.5,
        -1: lane_roll(ghost_y, -16 * WET_SLOT) > 0.5,
    }
    wet_z = {
        1: lane_roll(ghost_z, 7 - WET_SLOT) > 0.5,
        -1: lane_roll(ghost_z, -WET_SLOT) > 0.5,
    }
    wet_x = {s: ghost_x[s][2 * WET_SLOT : 2 * WET_SLOT + 2, :] > 0.5 for s in (1, -1)}
    put(0, jnp.where(wet, own_ref[0], 0.0), None)
    for i in range(1, 19):
        c = VELOCITIES[i]
        a = own_ref[i]
        if c[0] != 0:
            j = outgoing(1 if c[0] > 0 else 0).index(i)
            at = 30 if c[0] > 0 else 0
            work_ref[i] = a
            work_ref[i, at : at + 2, :] = jnp.where(
                wet_x[c[0]], ghost_x[c[0]][2 * j : 2 * j + 2, :], BIG
            )
            a = work_ref[i]
        if c[1] != 0:
            j = outgoing(3 if c[1] > 0 else 2).index(i)
            ghost = lane_roll(ghost_y, 112 - 16 * j if c[1] > 0 else -16 * j)
            fine = wet_y[c[1]]
            if c[0] != 0:
                fine = fine & grid.beyond(1, c[1], 0, c[0])
            a = jnp.where(grid.plane(1, c[1]), jnp.where(fine, ghost, BIG), a)
        if c[2] != 0:
            j = outgoing(5 if c[2] > 0 else 4).index(i)
            ghost = lane_roll(ghost_z, 7 - j if c[2] > 0 else -j)
            fine = wet_z[c[2]]
            for other in (0, 1):
                if c[other] != 0:
                    fine = fine & grid.beyond(2, c[2], other, c[other])
            a = jnp.where(grid.plane(2, c[2]), jnp.where(fine, ghost, BIG), a)
        moved = flat_roll(grid, a, sum(c[d] * STRIDES[d] for d in range(3)))
        open_link = moved < LIMIT
        value = jnp.where(open_link, moved, own_ref[OPPOSITE[i]])
        put(i, jnp.where(wet, value, 0.0), open_link)


def first_kernel(pop_ref, fluid_ref, post_ref, pack_ref):
    grid = Grid()
    wet = fluid_ref[...] > 0
    g = collide([pop_ref[i] for i in range(19)], wet)
    for i in range(19):
        post_ref[i] = jnp.where(wet, g[i], BIG)
    write_pack(grid, g, wet, pack_ref)


def middle_kernel(own_ref, fluid_ref, nb_ref, p0, p1, p2, p3, post_ref, pack_ref, sum_hbm, work_ref, now_ref, sign_ref, sum_ref, sem):
    grid = Grid()
    wet = fluid_ref[...] > 0

    def put(i, value, open_link):
        now_ref[i] = value
        if i:
            sign_ref[i] = jnp.where(wet, jnp.where(open_link, 1.0, -1.0), 0.0)

    me = place()
    tiles = (
        (other_side(me), p0),
        (pair_mate(me), p1),
        (other_side(pair_mate(me)), p2),
        (pair_mate(other_side(me)), p3),
    )
    pull(grid, wet, own_ref, nb_ref, tiles, None, work_ref, put)
    g = collide([now_ref[i] for i in range(19)], wet)
    totals = [None] * 3
    for i in range(1, 19, 2):
        signed = (g[i] * sign_ref[i + 1] - g[i + 1] * sign_ref[i]) * WEIGHTS[i]
        for dim in range(3):
            c = VELOCITIES[i][dim]
            if c > 0:
                totals[dim] = signed if totals[dim] is None else totals[dim] + signed
            elif c < 0:
                totals[dim] = -signed if totals[dim] is None else totals[dim] - signed
    lane = lax.broadcasted_iota(jnp.int32, sum_ref.shape, 2)
    line = jnp.zeros(sum_ref.shape, jnp.float32)
    for dim in range(3):
        total = jnp.sum(jnp.sum(totals[dim], axis=0, keepdims=True), axis=1, keepdims=True)[None]
        line = jnp.where(lane == dim, total, line)
    sum_ref[...] = line
    sum_copy = pltpu.make_async_copy(sum_ref, sum_hbm, sem)
    sum_copy.start()
    for i in range(19):
        post_ref[i] = jnp.where(wet, g[i], BIG)
    write_pack(grid, g, wet, pack_ref)
    sum_copy.wait()


def pick_kernel(nb_ref, p0, p1, p3, tile_ref):
    me = place()
    tiles = ((other_side(me), p0), (pair_mate(me), p1), (pair_mate(other_side(me)), p3))
    ghost_y, ghost_z, low_x, high_x = pick(Grid(), nb_ref, tiles)
    tile_ref[Y_AT : Y_AT + ROWS, :] = ghost_y
    tile_ref[Z_AT : Z_AT + ROWS, :] = ghost_z
    tile_ref[X_HIGH_AT : X_HIGH_AT + 12, :] = low_x
    tile_ref[X_LOW_AT : X_LOW_AT + 12, :] = high_x


def last_kernel(own_ref, fluid_ref, nb_ref, base_ref, p2, out_ref, work_ref):
    grid = Grid()
    wet = fluid_ref[...] > 0

    def put(i, value, open_link):
        out_ref[i] = value

    pull(grid, wet, own_ref, nb_ref, ((other_side(pair_mate(place())), p2),), base_ref, work_ref, put)


def vmem(count):
    return [pl.BlockSpec(memory_space=pltpu.VMEM)] * count


def swap(pack, partner):
    length = lax.axis_size("node") * lax.axis_size("local")
    pairs = [(i, partner(i)) for i in range(length) if 0 <= partner(i) < length]
    return lax.ppermute(pack, ("node", "local"), pairs)


def exchange(pack):
    other = swap(pack, other_side)
    mate = swap(pack, pair_mate)
    return [other, mate]


def pass_on(other, mate):
    past_mate = swap(other, pair_mate)
    past_other = swap(mate, other_side)
    return [other, mate, past_mate, past_other]


CORES = 2


def spread_out(lines, groups):
    return lax.all_to_all(lines, ("node", "local"), 0, 0, tiled=True, axis_index_groups=groups)


def shards(populations, fluid, neighbours):
    f32 = jnp.float32
    cube = jax.ShapeDtypeStruct((19, ROWS, LANES), f32)
    packed = jax.ShapeDtypeStruct((PACK_ROWS, LANES), f32)
    layer = CORES * lax.axis_size("local")
    layers = lax.axis_size("node") // CORES
    in_layer = [[z * layer + i for i in range(layer)] for z in range(layers)]
    across_layers = [[z * layer + i for z in range(layers)] for i in range(layer)]
    lines = jax.ShapeDtypeStruct((layer, 1, 3 * LANES), f32)
    scratch = pltpu.VMEM((19, ROWS, LANES), f32)
    smem = [pl.BlockSpec(memory_space=pltpu.SMEM)]
    devices = lax.axis_size("node") * lax.axis_size("local")
    params = pltpu.CompilerParams(vmem_limit_bytes=16 * 2**20)
    pop = populations.reshape(19, ROWS, LANES)
    wall = fluid.reshape(ROWS, LANES)

    post, pack = pl.pallas_call(
        first_kernel,
        out_shape=(cube, packed),
        in_specs=vmem(2),
        out_specs=tuple(vmem(2)),
        compiler_params=params,
        name="collide_first",
    )(pop, wall)
    ghosts = pass_on(*exchange(pack))
    post, pack, sums = pl.pallas_call(
        middle_kernel,
        out_shape=(cube, packed, lines),
        in_specs=vmem(2) + smem + vmem(4),
        out_specs=tuple(vmem(2)) + (pl.BlockSpec(memory_space=pl.ANY),),
        scratch_shapes=[scratch] * 3 + [pltpu.VMEM(lines.shape, f32), pltpu.SemaphoreType.DMA],
        compiler_params=params,
        name="stream_collide",
    )(post, wall, neighbours, *ghosts)
    sums = spread_out(sums, in_layer)
    other, mate = exchange(pack)
    sums, mate = lax.optimization_barrier((sums, mate))
    plane = jnp.sum(sums[:, 0, :LANES], axis=0)[None, None]
    sums = spread_out(jnp.broadcast_to(plane, (layers, 2, LANES)), across_layers)
    other, mate, past_mate, past_other = pass_on(other, mate)
    tile = pl.pallas_call(
        pick_kernel,
        out_shape=packed,
        in_specs=smem + vmem(3),
        out_specs=vmem(1)[0],
        compiler_params=params,
        name="pick_tiles",
        cost_estimate=pl.CostEstimate(flops=1000000, bytes_accessed=400000, transcendentals=0),
    )(neighbours, other, mate, past_other)
    out = pl.pallas_call(
        last_kernel,
        out_shape=cube,
        in_specs=vmem(2) + smem + vmem(2),
        out_specs=vmem(1)[0],
        scratch_shapes=[scratch],
        compiler_params=params,
        name="stream_last",
        cost_estimate=pl.CostEstimate(flops=4000000, bytes_accessed=1000000, transcendentals=0),
    )(post, wall, neighbours, tile, past_mate)
    flow = jnp.sum(sums[:, 0, :3], axis=0) / (devices * BLK * BLK)
    return out.reshape(populations.shape), flow


def solution(mesh):
    in_specs = (
        P(("node", "local"), None, None),
        P(("node", "local"), None),
        P(("node", "local"), None),
    )
    out_specs = (P(("node", "local"), None, None), P())
    return jax.shard_map(shards, mesh=mesh, in_specs=in_specs, out_specs=out_specs, check_vma=False)
```
